512 devices in a mesh: loop: 16 (over z_hi, x, core), rep: 32 (over z_lo, y).
Axes of the slice: x: 4, y: 4, z: 16 (z_hi: 2, z_lo: 8; z = z_hi * 8 + z_lo), core: 2. Of those that a mesh axis runs over, the one named last changes fastest.
Arguments:
- features: bfloat16 [3072, 32, 1152], P('loop', 'rep'), may hold values from -6 to 6
- text: bfloat16 [3072, 32, 1152], P('loop', 'rep'), may hold values from -6 to 6
- proj: bfloat16 [1152, 1152], replicated, may hold values from -0.1875 to 0.1875
- gain: float32 [1152], replicated, may hold values from 0.5 to 1.5
- scale: float32 [1], replicated, may hold values from 8 to 32
- bias: float32 [1], replicated, may hold values from -4 to 0
Outputs:
- feature_grad: bfloat16 [3072, 32, 1152], P('loop', 'rep')
- text_grad: bfloat16 [3072, 32, 1152], P('loop', 'rep')
- proj_grad: float32 [1152, 1152], P('rep')
- gain_gradient: float32 [1152], replicated
The draws below stay inside these ranges and needn't reach their ends.
All inputs are finite; a program needn't handle non-finite values.
Results may differ from the reference program's by a relative error of at most 0.024.
Values may be sent and summed in bfloat16 or wider, within the bound.
A program may use at most 64 MiB of HBM per device.

```python
import math
import jax
import jax.numpy as jnp
from jax import lax

W = 1152
E = 1152
ROWS_DEV = 192
PAIRS_PER_GROUP = 3072
GROUPS = 32
N_LOOP = 16


def with_spikes(entries, rng, source, target, shards_of, factor):
    def block_of(dim):
        return (jnp.arange(entries.shape[dim]) // (entries.shape[dim] // shards_of)).reshape((-1,) + (1,) * (entries.ndim - 1 - dim))

    first = jax.random.permutation(rng, shards_of)[block_of(target)]
    other_side = (block_of(target) + shards_of // 2) % shards_of
    return jnp.where((block_of(source) == first) | (block_of(source) == other_side), factor * entries, entries)


def block_levels(own_key, extent, cuts, low, high):
    loudness = 1.0
    for axis_at, blocks in cuts:
        draws = jax.random.uniform(jax.random.fold_in(jax.random.fold_in(own_key, 6), axis_at), (blocks,), jnp.float32, low / len(cuts), high / len(cuts))
        loudness = loudness * jnp.repeat(jnp.exp(draws), extent[axis_at] // blocks).reshape((-1,) + (1,) * (len(extent) - 1 - axis_at))
    return loudness


def centred(stream_key, extent, spread, limit, shards=(), kind=jnp.bfloat16):
    factor_of = block_levels(stream_key, extent, shards, -0.22, 0.18) if shards else 1.0
    array = jax.random.normal(stream_key, extent, jnp.float32) * spread * factor_of
    return jnp.minimum(jnp.maximum(array, -limit), limit).astype(kind)


def gaussian_with(rng, dims, scale, most, shards, heavy, kind=jnp.bfloat16):
    values = scale * jax.random.normal(rng, dims, jnp.float32)
    if shards:
        values = values * block_levels(rng, dims, shards, -0.22, 0.18)
    return jnp.clip(with_spikes(values, jax.random.fold_in(rng, 3), *heavy), -most, most).astype(kind)


def setup_inputs(seed: int = 0) -> dict:
    keys = jax.random.split(jax.random.key(seed), 7)
    return {
        "features": gaussian_with(keys[0], (PAIRS_PER_GROUP, GROUPS, W), 1.0, 6.0, ((0, 16), (1, 32)), (1, 2, 32, 2.75)),
        "text": centred(keys[1], (PAIRS_PER_GROUP, GROUPS, E), 1.0, 6.0, ((0, 16), (1, 32))),
        "proj": centred(keys[2], (W, E), W ** -0.5, 0.1875),
        "gain": jnp.clip(1.0 + 0.1 * jax.random.normal(keys[3], (W,), jnp.float32), 0.5, 1.5),
        "scale": jnp.clip(jnp.exp(jax.random.uniform(keys[4], (1,), jnp.float32, math.log(8.0), math.log(32.0))), 8.0, 32.0),
        "bias": jnp.clip(jax.random.uniform(keys[5], (1,), jnp.float32, -4.0, 0.0), -4.0, 0.0),
    }


def unit_rows(values):
    inverse = lax.rsqrt(lax.optimization_barrier(jnp.sum(values * values, axis=-1, keepdims=True)) + 1e-06)
    return (values * inverse, inverse)

def reference(features, text, proj, gain, scale, bias):
    logit_scale = scale[0]
    logit_bias = bias[0]
    diag_mask = jnp.eye(PAIRS_PER_GROUP, dtype=jnp.float32)

    def group_pass(carry, inputs):
        proj_sum, gain_total = carry
        image_rows, text_rows = inputs
        xvalues = image_rows.astype(jnp.float32)
        row_mean = lax.optimization_barrier(jnp.mean(xvalues, axis=-1, keepdims=True))
        mean_removed = xvalues - row_mean
        row_inverse_deviation = lax.rsqrt(lax.optimization_barrier(jnp.mean(mean_removed * mean_removed, axis=-1, keepdims=True)) + 1e-06)
        standardized_input = mean_removed * row_inverse_deviation
        normalized_rows = (standardized_input * gain).astype(jnp.bfloat16)
        projected = jnp.dot(normalized_rows, proj, preferred_element_type=jnp.float32)
        img_dir, img_inv = unit_rows(projected)
        img_unit = img_dir.astype(jnp.bfloat16)
        txt_dir, txt_inv = unit_rows(text_rows.astype(jnp.float32))
        txt_unit = txt_dir.astype(jnp.bfloat16)
        logits = logit_scale * jnp.dot(img_unit, txt_unit.T, preferred_element_type=jnp.float32) + logit_bias
        pair_weight = (jax.nn.sigmoid(logits) - diag_mask).astype(jnp.bfloat16)
        img_back = logit_scale * jnp.dot(pair_weight, txt_unit, preferred_element_type=jnp.float32)
        txt_back = logit_scale * jnp.dot(pair_weight.T, img_unit, preferred_element_type=jnp.float32)
        proj_back = ((img_back - img_dir * lax.optimization_barrier(jnp.sum(img_dir * img_back, axis=-1, keepdims=True))) * img_inv).astype(jnp.bfloat16)
        text_out = ((txt_back - txt_dir * lax.optimization_barrier(jnp.sum(txt_dir * txt_back, axis=-1, keepdims=True))) * txt_inv).astype(jnp.bfloat16)
        norm_backward = jnp.dot(proj_back, proj.T, preferred_element_type=jnp.float32)
        scaled_backward = norm_backward * gain
        feature_result = (row_inverse_deviation * (scaled_backward - lax.optimization_barrier(jnp.mean(scaled_backward, axis=-1, keepdims=True)) - standardized_input * lax.optimization_barrier(jnp.mean(scaled_backward * standardized_input, axis=-1, keepdims=True)))).astype(jnp.bfloat16)
        normed_blocks = normalized_rows.astype(jnp.float32).reshape(N_LOOP, ROWS_DEV, W)
        back_blocks = proj_back.astype(jnp.float32).reshape(N_LOOP, ROWS_DEV, E)
        partials = jnp.einsum('lrw,lre->lwe', normed_blocks, back_blocks, precision=lax.Precision.HIGHEST) / PAIRS_PER_GROUP
        partials = lax.optimization_barrier(partials.astype(jnp.bfloat16))
        proj_sum = proj_sum + lax.optimization_barrier(jnp.sum(partials.astype(jnp.float32), axis=0))
        gain_total = gain_total + lax.optimization_barrier(jnp.sum(norm_backward * standardized_input, axis=0)) / PAIRS_PER_GROUP
        return ((proj_sum, gain_total), (feature_result, text_out))
    start = (jnp.zeros((W, E), jnp.float32), jnp.zeros((W,), jnp.float32))
    (proj_grad, gain_gradient), (feature_all, text_all) = lax.scan(group_pass, start, (jnp.transpose(features, (1, 0, 2)), jnp.transpose(text, (1, 0, 2))))
    feature_grad = jnp.transpose(feature_all, (1, 0, 2))
    text_grad = jnp.transpose(text_all, (1, 0, 2))
    return (feature_grad, text_grad, proj_grad, gain_gradient)
```

```python
import functools

import jax
import jax.numpy as jnp
from jax import lax
from jax.experimental import pallas as pl
from jax.experimental.pallas import tpu as pltpu
from jax.sharding import PartitionSpec as P

MESH = pl.DeviceIdType.MESH
WIDTH = 1152
ROWS = 192
CHUNK = 48
CHUNKS = ROWS // CHUNK
PAIRS = 3072
TXT, IMG = 0, 1
OWN, FAR = 0, 1
WINDOW = 3
BLOCK_ROWS = 144
PIECE = 48
CUT = 640
LAST = (((1,), (1,)), ((), ()))
FIRST = (((0,), (0,)), ((), ()))
F32 = jnp.float32
BF16 = jnp.bfloat16


def coordinates():
    loop = lax.axis_index("loop")
    rep = lax.axis_index("rep")
    x = (loop // 2) % 4
    core = loop % 2
    z = (loop // 8) * 8 + rep // 4
    y = rep % 4
    return x, y, z, core


def device(x, y, z, core):
    x = (x + 4) % 4
    y = (y + 4) % 4
    z = (z + 32) % 16
    return ((z // 8) * 8 + x * 2 + core, (z % 8) * 4 + y)


def remote(src, dst, send_sem, recv_sem, target):
    return pltpu.make_async_remote_copy(
        src_ref=src,
        dst_ref=dst,
        send_sem=send_sem,
        recv_sem=recv_sem,
        device_id=target,
        device_id_type=MESH,
    )


def greet(peers):
    barrier = pltpu.get_barrier_semaphore()
    for peer in peers:
        pl.semaphore_signal(barrier, 1, device_id=peer, device_id_type=MESH)
    return lambda: pl.semaphore_wait(barrier, len(peers))


def row_sum(values):
    return jnp.sum(values, axis=-1, keepdims=True)


def pair_kernel(
    feat_ref, text_ref, proj_ref, gain_ref, scale_ref, bias_ref,
    feature_out, text_out, partial_out, gain_out,
    units, acc, xhat_ref, normed_ref, img_dir_ref, txt_dir_ref, row_ref,
    x_send, x_recv, s_send, s_recv, z_send, z_recv,
):
    x, y, z, core = coordinates()
    mine = x * 2 + core
    sibling = device(x, y, z, 1 - core)
    plus, minus = device(x + 1, y, z, core), device(x - 1, y, z, core)
    far = device(x, y, z + 8, core)
    finish_barrier = greet([sibling, plus, minus, far])
    scale = scale_ref[0]
    bias = bias_ref[0]

    def slot(steps, other=0):
        owner_core = core if other == 0 else 1 - core
        return ((x + steps) % 4) * 2 + owner_core

    def x_copy(arr, half, k, steps, src_slot, target):
        block = units.at[arr, half, k, src_slot]
        return remote(block, block, x_send.at[arr, half, k, steps], x_recv.at[arr, half, k, steps], target)

    def s_copy(arr, half, k, steps, from_sibling=0):
        block = units.at[arr, half, k, slot(steps, from_sibling)]
        return remote(block, block, s_send.at[arr, half, k, steps], s_recv.at[arr, half, k, steps], sibling)

    def z_copy(arr, k):
        return remote(
            units.at[arr, OWN, k, mine], units.at[arr, FAR, k, mine], z_send.at[arr, k], z_recv.at[arr, k], far
        )

    def plus_copy(arr, half, k):
        return x_copy(arr, half, k, 3, mine, plus)

    def minus_copy(arr, half, k):
        return x_copy(arr, half, k, 1, mine, minus)

    def onward_copy(arr, half, k):
        even = (k % 2) == 0
        steps = jnp.where(even, 3, 1)
        loop_id = jnp.where(even, plus[0], minus[0])
        return x_copy(arr, half, k, 2, slot(steps), (loop_id, plus[1]))

    def recv_x(arr, half, k, steps):
        x_copy(arr, half, k, steps, slot(steps), plus).wait_recv()

    def spread_own(arr, half, k):
        plus_copy(arr, half, k).start()
        minus_copy(arr, half, k).start()
        s_copy(arr, half, k, 0).start()

    def spread_neighbours(arr, half, k):
        recv_x(arr, half, k, 3)
        recv_x(arr, half, k, 1)
        onward_copy(arr, half, k).start()
        s_copy(arr, half, k, 3).start()
        s_copy(arr, half, k, 1).start()

    def spread_last(arr, half, k):
        recv_x(arr, half, k, 2)
        s_copy(arr, half, k, 2).start()

    def wait_sibling(arr, half, k):
        for steps in range(4):
            s_copy(arr, half, k, steps, 1).wait_recv()

    def wait_sends(arr, half, k):
        plus_copy(arr, half, k).wait_send()
        minus_copy(arr, half, k).wait_send()
        onward_copy(arr, half, k).wait_send()
        for steps in range(4):
            s_copy(arr, half, k, steps).wait_send()

    def attend(arr, half, k):
        own = units[1 - arr, OWN, :, mine].reshape(ROWS, WIDTH)
        keys = units[arr, half, k].reshape(8 * CHUNK, WIDTH)
        logits = scale * lax.dot_general(own, keys, LAST, preferred_element_type=F32) + bias
        weight = jax.nn.sigmoid(logits)
        if half == OWN:
            row = lax.broadcasted_iota(jnp.int32, weight.shape, 0)
            col = lax.broadcasted_iota(jnp.int32, weight.shape, 1)
            on = (col - mine * CHUNK == row - k * CHUNK) & (row >= k * CHUNK) & (row < (k + 1) * CHUNK)
            weight = weight - jnp.where(on, 1.0, 0.0)
        weight = weight.astype(BF16)
        acc[arr] += scale * jnp.dot(weight, keys, preferred_element_type=F32)

    def each(count, body):
        def step(k, carry):
            body(k)
            return carry

        lax.fori_loop(0, count, step, 0)

    acc[...] = jnp.zeros_like(acc)
    values = text_ref[...].astype(F32)
    txt_inv = lax.rsqrt(row_sum(values * values) + 1e-6)
    txt_dir = values * txt_inv
    txt_dir_ref[...] = txt_dir
    units[TXT, OWN, :, mine] = txt_dir.astype(BF16).reshape(CHUNKS, CHUNK, WIDTH)
    row_ref[0] = jnp.broadcast_to(txt_inv, (ROWS, 128))
    finish_barrier()
    for k in range(WINDOW):
        z_copy(TXT, k).start()
    each(CHUNKS, lambda k: spread_own(TXT, OWN, k))

    values = feat_ref[...].astype(F32)
    centred = values - row_sum(values) * (1.0 / WIDTH)
    deviation = lax.rsqrt(row_sum(centred * centred) * (1.0 / WIDTH) + 1e-6)
    row_ref[1] = jnp.broadcast_to(deviation, (ROWS, 128))
    xhat = centred * deviation
    xhat_ref[...] = xhat
    normed_ref[...] = (xhat * gain_ref[...]).astype(BF16)
    projected = jnp.dot(normed_ref[...], proj_ref[...], preferred_element_type=F32)
    img_inv = lax.rsqrt(row_sum(projected * projected) + 1e-6)
    row_ref[2] = jnp.broadcast_to(img_inv, (ROWS, 128))
    img_dir = projected * img_inv
    img_dir_ref[...] = img_dir
    units[IMG, OWN, :, mine] = img_dir.astype(BF16).reshape(CHUNKS, CHUNK, WIDTH)

    each(CHUNKS, lambda k: spread_neighbours(TXT, OWN, k))
    each(CHUNKS, lambda k: spread_last(TXT, OWN, k))

    def own_text(k):
        spread_own(IMG, OWN, k)
        wait_sibling(TXT, OWN, k)
        attend(TXT, OWN, k)

    each(CHUNKS, own_text)

    def far_text(k):
        z_copy(TXT, k).wait_recv()
        ahead = k + WINDOW

        @pl.when(ahead < CHUNKS)
        def _():
            z_copy(TXT, jnp.minimum(ahead, CHUNKS - 1)).start()

        @pl.when(ahead >= CHUNKS)
        def _():
            z_copy(IMG, jnp.maximum(ahead - CHUNKS, 0)).start()

        spread_own(TXT, FAR, k)
        spread_neighbours(IMG, OWN, k)
        spread_neighbours(TXT, FAR, k)
        spread_last(IMG, OWN, k)
        spread_last(TXT, FAR, k)
        wait_sibling(TXT, FAR, k)
        attend(TXT, FAR, k)
        wait_sibling(IMG, OWN, k)
        attend(IMG, OWN, k)

    each(CHUNKS, far_text)

    img_back = acc[TXT]
    img_dir = img_dir_ref[...]
    img_inv = row_ref[2][:, :1]
    proj_back = ((img_back - img_dir * row_sum(img_dir * img_back)) * img_inv).astype(BF16)
    partial = lax.dot_general(normed_ref[...], proj_back, FIRST, preferred_element_type=F32)
    partial_out[...] = (partial * (1.0 / PAIRS)).astype(BF16)
    norm_back = lax.dot_general(proj_back, proj_ref[...], LAST, preferred_element_type=F32)
    xhat = xhat_ref[...]
    deviation = row_ref[1][:, :1]
    gain_terms = (norm_back * xhat).reshape(ROWS // 8, 8, WIDTH)
    gain_out[...] = jnp.sum(gain_terms, axis=0) * (1.0 / PAIRS)
    scaled = norm_back * gain_ref[...]
    mean = row_sum(scaled) * (1.0 / WIDTH)
    along = row_sum(scaled * xhat) * (1.0 / WIDTH)
    feature_out[...] = (deviation * (scaled - mean - xhat * along)).astype(BF16)

    def far_image(k):
        z_copy(IMG, k).wait_recv()

        @pl.when(k + WINDOW < CHUNKS)
        def _():
            z_copy(IMG, jnp.minimum(k + WINDOW, CHUNKS - 1)).start()

        spread_own(IMG, FAR, k)
        spread_neighbours(IMG, FAR, k)
        spread_last(IMG, FAR, k)
        wait_sibling(IMG, FAR, k)
        attend(IMG, FAR, k)

    each(CHUNKS, far_image)

    txt_back = acc[IMG]
    txt_dir = txt_dir_ref[...]
    txt_inv = row_ref[0][:, :1]
    text_out[...] = ((txt_back - txt_dir * row_sum(txt_dir * txt_back)) * txt_inv).astype(BF16)

    def drain(k):
        for arr in (TXT, IMG):
            z_copy(arr, k).wait_send()
            for half in (OWN, FAR):
                wait_sends(arr, half, k)

    each(CHUNKS, drain)


def reduce_kernel(
    partial_ref, gain_ref, grad_out, gain_out,
    s_buf, summed, y_buf, y_sum, x_buf, x_sum, z_buf, gathered, g_sum, g_buf,
    s_send, s_recv, y_send, y_recv, x_send, x_recv, z_send, z_recv,
    b_send, b_recv, g_send, g_recv,
):
    x, y, z, core = coordinates()
    sibling = device(x, y, z, 1 - core)
    x_peers = [device(x + d, y, z, core) for d in (1, 2, 3)]
    y_peers = [device(x, y + d, z, core) for d in (1, 2, 3)]
    z_peers = [device(x, y, z + d, core) for d in range(1, 16)]
    greet([sibling] + x_peers + y_peers + z_peers)()

    def g_copies(stage, peers, base):
        return [
            remote(g_sum.at[stage], g_buf.at[base + i], g_send.at[base + i], g_recv.at[base + i], peer)
            for i, peer in enumerate(peers)
        ]

    def g_begin(stage, peers, base):
        for copy in g_copies(stage, peers, base):
            copy.start()

    def g_end(stage, peers, base):
        total = g_sum[stage]
        for i, copy in enumerate(g_copies(stage, peers, base)):
            copy.wait()
            total = total + g_buf[base + i]
        g_sum[stage + 1] = total

    z_quad = [device(x, y, z + 4 * d, core) for d in (1, 2, 3)]
    z_near = [device(x, y, (z // 4) * 4 + (z + d) % 4, core) for d in (1, 2, 3)]
    stages = [([sibling], 0), (y_peers, 1), (x_peers, 4), (z_quad, 7), (z_near, 10)]

    g_sum[0] = gain_ref[...]
    for j in range(4):
        rows = pl.ds(pl.multiple_of((1 - core) * 576 + j * BLOCK_ROWS, 16), BLOCK_ROWS)
        remote(partial_ref.at[rows], s_buf.at[j], s_send.at[j], s_recv.at[j], sibling).start()
    g_begin(0, *stages[0])

    def s_wait(j):
        return remote(partial_ref.at[pl.ds(0, BLOCK_ROWS)], s_buf.at[j], s_send.at[j], s_recv.at[j], sibling)

    def y_copy(j, d):
        rows = pl.ds(pl.multiple_of(((y + d) % 4) * 32, 16), PIECE)
        return remote(summed.at[j, rows], y_buf.at[d - 1, j], y_send.at[d - 1, j], y_recv.at[d - 1, j], y_peers[d - 1])

    for j in range(4):
        s_wait(j).wait_recv()
        rows = pl.ds(pl.multiple_of(core * 576 + j * BLOCK_ROWS, 16), BLOCK_ROWS)
        summed[j] = (partial_ref[rows].astype(F32) + s_buf[j].astype(F32)).astype(BF16)
        for d in (1, 2, 3):
            y_copy(j, d).start()
    g_end(0, *stages[0])
    g_begin(1, *stages[1])
    g_end(1, *stages[1])
    g_begin(2, *stages[2])

    here = pl.ds(pl.multiple_of(y * 32, 16), PIECE)
    for j in range(4):
        total = summed[j, here].astype(F32)
        for d in (1, 2, 3):
            y_copy(j, d).wait_recv()
            total = total + y_buf[d - 1, j].astype(F32)
        y_sum[j] = total.astype(BF16)

        @pl.when(x != j)
        def _():
            d = (j - x + 4) % 4
            remote(
                y_sum.at[j], x_buf.at[d - 1], x_send.at[d - 1], x_recv.at[d - 1], (device(j, y, z, core))
            ).start()

    g_end(2, *stages[2])
    g_begin(3, *stages[3])

    def x_wait(d):
        return remote(y_sum.at[0], x_buf.at[d - 1], x_send.at[d - 1], x_recv.at[d - 1], x_peers[0])

    total = y_sum[x].astype(F32)
    for d in (1, 2, 3):
        x_wait(d).wait_recv()
        total = total + x_buf[d - 1].astype(F32)
    x_sum[...] = total.astype(BF16)

    holder = core * 4 + x
    low, high = pl.ds(0, CUT), pl.ds(CUT, WIDTH - CUT)

    def z_copy(half, away):
        cols = low if half == 0 else high
        size = CUT if half == 0 else WIDTH - CUT
        return remote(
            x_sum.at[:, cols], z_buf.at[away - 1, :, pl.ds(0, size)], z_send.at[half], z_recv.at[away - 1],
            device(x, y, holder + 8 * half, core),
        )

    for half in (0, 1):
        away = (z - holder - 8 * half + 32) % 16

        @pl.when(away != 0)
        def _():
            z_copy(half, away).start()

    g_end(3, *stages[3])
    g_begin(4, *stages[4])

    def b1_copy(half):
        cols = low if half == 0 else high
        return remote(
            gathered.at[:, cols], gathered.at[:, cols], b_send.at[0], b_recv.at[0], device(x, y, z + 8, core)
        )

    is_holder = (z % 8) == holder
    for half in (0, 1):

        @pl.when(is_holder & (z // 8 == half))
        def _():
            size = CUT if half == 0 else WIDTH - CUT
            cols = low if half == 0 else high
            total = x_sum[:, cols].astype(F32)
            for away in range(1, 16):
                z_copy(half, away).wait_recv()
                total = total + z_buf[away - 1, :, pl.ds(0, size)].astype(F32)
            gathered[:, cols] = total.astype(BF16)
            b1_copy(half).start()
            b1_copy(1 - half).wait_recv()
            b1_copy(half).wait_send()

    def b2_copy(i):
        return remote(gathered, gathered, b_send.at[1 + i], b_recv.at[1], x_peers[i])

    def b3_copy():
        return remote(gathered, gathered, b_send.at[4], b_recv.at[1], sibling)

    root_core = (z % 8) // 4

    @pl.when(is_holder)
    def _():
        for i in range(3):
            b2_copy(i).start()

    @pl.when(jnp.logical_not(is_holder))
    def _():
        b2_copy(0).wait_recv()

    @pl.when(core == root_core)
    def _():
        b3_copy().start()

    g_end(4, *stages[4])
    gain_out[...] = jnp.sum(g_sum[5], axis=0, keepdims=True)

    @pl.when(is_holder)
    def _():
        for i in range(3):
            b2_copy(i).wait_send()

    @pl.when(core == root_core)
    def _():
        b3_copy().wait_send()

    grad_out[...] = gathered[...].astype(F32)
    for j in range(4):
        s_wait(j).wait_send()
        for d in (1, 2, 3):
            y_copy(j, d).wait_send()
    for d in (1, 2, 3):
        x_wait(d).wait_send()
    for half in (0, 1):
        away = (z - holder - 8 * half + 32) % 16

        @pl.when(away != 0)
        def _():
            z_copy(half, away).wait_send()


def local(features, text, proj, gain, scale, bias):
    vmem = pl.BlockSpec(memory_space=pltpu.VMEM)
    smem = pl.BlockSpec(memory_space=pltpu.SMEM)
    dma = pltpu.SemaphoreType.DMA
    feature_grad, text_grad, partial, gain_part = pl.pallas_call(
        pair_kernel,
        out_shape=[
            jax.ShapeDtypeStruct((ROWS, WIDTH), BF16),
            jax.ShapeDtypeStruct((ROWS, WIDTH), BF16),
            jax.ShapeDtypeStruct((WIDTH, WIDTH), BF16),
            jax.ShapeDtypeStruct((8, WIDTH), F32),
        ],
        in_specs=[vmem] * 4 + [smem] * 2,
        out_specs=[vmem] * 4,
        scratch_shapes=[
            pltpu.VMEM((2, 2, CHUNKS, 8, CHUNK, WIDTH), BF16),
            pltpu.VMEM((2, ROWS, WIDTH), F32),
            pltpu.VMEM((ROWS, WIDTH), F32),
            pltpu.VMEM((ROWS, WIDTH), BF16),
            pltpu.VMEM((ROWS, WIDTH), F32),
            pltpu.VMEM((ROWS, WIDTH), F32),
            pltpu.VMEM((3, ROWS, 128), F32),
            dma((2, 2, CHUNKS, 4)),
            dma((2, 2, CHUNKS, 4)),
            dma((2, 2, CHUNKS, 4)),
            dma((2, 2, CHUNKS, 4)),
            dma((2, CHUNKS)),
            dma((2, CHUNKS)),
        ],
        compiler_params=pltpu.CompilerParams(
            collective_id=0, has_side_effects=True, vmem_limit_bytes=60 * 2**20
        ),
        name="pairs",
    )(features[:, 0, :], text[:, 0, :], proj, gain[None, :], scale, bias)
    grad, gain_gradient = pl.pallas_call(
        reduce_kernel,
        out_shape=[
            jax.ShapeDtypeStruct((PIECE, WIDTH), F32),
            jax.ShapeDtypeStruct((1, WIDTH), F32),
        ],
        in_specs=[vmem] * 2,
        out_specs=[vmem] * 2,
        scratch_shapes=[
            pltpu.VMEM((4, BLOCK_ROWS, WIDTH), BF16),
            pltpu.VMEM((4, BLOCK_ROWS, WIDTH), BF16),
            pltpu.VMEM((3, 4, PIECE, WIDTH), BF16),
            pltpu.VMEM((4, PIECE, WIDTH), BF16),
            pltpu.VMEM((3, PIECE, WIDTH), BF16),
            pltpu.VMEM((PIECE, WIDTH), BF16),
            pltpu.VMEM((15, PIECE, CUT), BF16),
            pltpu.VMEM((PIECE, WIDTH), BF16),
            pltpu.VMEM((6, 8, WIDTH), F32),
            pltpu.VMEM((13, 8, WIDTH), F32),
            dma((4,)),
            dma((4,)),
            dma((3, 4)),
            dma((3, 4)),
            dma((3,)),
            dma((3,)),
            dma((2,)),
            dma((15,)),
            dma((5,)),
            dma((2,)),
            dma((13,)),
            dma((13,)),
        ],
        compiler_params=pltpu.CompilerParams(
            collective_id=1, has_side_effects=True, vmem_limit_bytes=60 * 2**20
        ),
        name="reduce",
    )(partial, gain_part)
    y = lax.axis_index("rep") % 4
    proj_grad = lax.dynamic_slice_in_dim(grad, y * 4, 36, 0)
    return feature_grad[:, None, :], text_grad[:, None, :], proj_grad, gain_gradient[0]


def solution(mesh):
    return jax.shard_map(
        local,
        mesh=mesh,
        in_specs=(P("loop", "rep", None), P("loop", "rep", None), P(), P(), P(), P()),
        out_specs=(P("loop", "rep", None), P("loop", "rep", None), P("rep", None), P()),
        check_vma=False,
    )
```

```python
import functools

import jax
import jax.numpy as jnp
from jax import lax
from jax.experimental import pallas as pl
from jax.experimental.pallas import tpu as pltpu
from jax.sharding import PartitionSpec as P

MESH = pl.DeviceIdType.MESH
WIDTH = 1152
ROWS = 192
GRAIN = 16
GRAINS = ROWS // GRAIN
CHUNKS = (4, 4, 3, 1)
STARTS = (0, 4, 8, 11)
COUNT = len(CHUNKS)
PAIRS = 3072
TXT, IMG = 0, 1
OWN, FAR = 0, 1
WINDOW = 3
BLOCK_ROWS = 144
PIECE = 48
CUT = 512
REST = WIDTH - CUT
LAST = (((1,), (1,)), ((), ()))
FIRST = (((0,), (0,)), ((), ()))
F32 = jnp.float32
BF16 = jnp.bfloat16


def coordinates():
    loop = lax.axis_index("loop")
    rep = lax.axis_index("rep")
    x = (loop // 2) % 4
    core = loop % 2
    z = (loop // 8) * 8 + rep // 4
    y = rep % 4
    return x, y, z, core


def device(x, y, z, core):
    x = (x + 4) % 4
    y = (y + 4) % 4
    z = (z + 32) % 16
    return ((z // 8) * 8 + x * 2 + core, (z % 8) * 4 + y)


def remote(src, dst, send_sem, recv_sem, target):
    return pltpu.make_async_remote_copy(
        src_ref=src,
        dst_ref=dst,
        send_sem=send_sem,
        recv_sem=recv_sem,
        device_id=target,
        device_id_type=MESH,
    )


def greet(peers):
    barrier = pltpu.get_barrier_semaphore()
    for peer in peers:
        pl.semaphore_signal(barrier, 1, device_id=peer, device_id_type=MESH)
    return lambda: pl.semaphore_wait(barrier, len(peers))


def row_sum(values):
    return jnp.sum(values, axis=-1, keepdims=True)

ONWARD = (1, -1, 1, -1)
TXT_OWN = ((5.3, 10.3, 13.0), (8.7, 13.7, 16.7), (11.2, 16.2, 19.0), (12.0, 17.0, 20.0))
IMG_OWN = ((13.1, 21.0, 27.0, 30.0), (21.1, 28.0, 34.0, 37.0), (31.0, 38.0, 43.0, 58.0), (43.5, 51.0, 56.0, 60.0))
FAR_TIMES = (
    ((15.2, 20.5, 25.0, 28.0), (28.4, 33.5, 38.0, 40.0), (38.3, 43.0, 46.0, 47.0), (41.6, 44.0, 46.5, 48.0)),
    ((54.9, 60.0, 64.5, 67.5), (68.1, 73.0, 77.5, 79.5), (78.0, 82.5, 85.5, 87.0), (81.3, 83.5, 86.0, 88.0)),
)
TAIL = (49.0, 53.0, 56.0, 66.5, 67.0, 70.5, 72.0, 82.0, 86.2, 89.0)
GAIN_TIMES = (59.0, 62.0, 65.0, 70.0, 75.0)


def pair_kernel(
    feat_ref, text_ref, proj_ref, gain_ref, scale_ref, bias_ref,
    feature_out, text_out, grad_out, gain_out,
    units, acc, xhat_ref, normed_ref, normed_t, img_dir_ref, txt_dir_ref, row_ref, back_ref,
    theirs, summed, s_buf, ya_buf, ya_sum, xb_buf, xb_sum, xa_buf, yb_buf, part, z_buf, gathered, g_sum, g_buf,
    x_send, x_recv, s_send, s_recv, z_send, z_recv,
    c_send, c_recv, ya_send, ya_recv, xb_send, xb_recv, xa_send, xa_recv, yb_send, yb_recv,
    h_send, h_recv, b_send, b_recv, g_send, g_recv,
):
    x, y, z, core = coordinates()
    mine = x * 2 + core
    sibling = device(x, y, z, 1 - core)
    plus, minus = device(x + 1, y, z, core), device(x - 1, y, z, core)
    x_peers = [plus, device(x + 2, y, z, core), minus]
    y_peers = [device(x, y + d, z, core) for d in (1, 2, 3)]
    z_peers = [device(x, y, z + d, core) for d in range(1, 16)]
    z_quad = [device(x, y, z + 4 * d, core) for d in (1, 2, 3)]
    z_near = [device(x, y, (z // 4) * 4 + (z + d) % 4, core) for d in (1, 2, 3)]
    far = z_peers[7]
    finish_barrier = greet([sibling] + x_peers + y_peers + z_peers)
    scale = scale_ref[0]
    bias = bias_ref[0]
    started = []

    def go(copy):
        copy.start()
        started.append(copy)

    def slot(steps, other=0):
        owner_core = core if other == 0 else 1 - core
        return ((x + steps) % 4) * 2 + owner_core

    def block(arr, half, k, where):
        return units.at[arr, half, pl.ds(STARTS[k], CHUNKS[k]), where]

    def x_copy(arr, half, k, steps, where, target):
        ref = block(arr, half, k, where)
        return remote(ref, ref, x_send.at[arr, half, k, steps], x_recv.at[arr, half, k, steps], target)

    def s_copy(arr, half, k, steps, from_sibling=0):
        ref = block(arr, half, k, slot(steps, from_sibling))
        return remote(ref, ref, s_send.at[arr, half, k, steps], s_recv.at[arr, half, k, steps], sibling)

    def z_copy(arr, k):
        return remote(block(arr, OWN, k, mine), block(arr, FAR, k, mine), z_send.at[arr, k], z_recv.at[arr, k], far)

    def recv_x(arr, half, k, steps):
        x_copy(arr, half, k, steps, slot(steps), plus).wait_recv()

    def spread_own(arr, half, k):
        go(x_copy(arr, half, k, 3, mine, plus))
        go(x_copy(arr, half, k, 1, mine, minus))
        go(s_copy(arr, half, k, 0))

    def spread_neighbours(arr, half, k):
        recv_x(arr, half, k, 3)
        recv_x(arr, half, k, 1)
        if ONWARD[k] == 1:
            go(x_copy(arr, half, k, 2, slot(3), plus))
        else:
            go(x_copy(arr, half, k, 2, slot(1), minus))
        go(s_copy(arr, half, k, 3))
        go(s_copy(arr, half, k, 1))

    def spread_last(arr, half, k):
        recv_x(arr, half, k, 2)
        go(s_copy(arr, half, k, 2))

    def attend(arr, half, k):
        for steps in range(4):
            s_copy(arr, half, k, steps, 1).wait_recv()
        first, count = STARTS[k], CHUNKS[k]
        own = units[1 - arr, OWN, :, mine].reshape(ROWS, WIDTH)
        keys = units[arr, half, pl.ds(first, count)].reshape(count * 8 * GRAIN, WIDTH)
        logits = scale * lax.dot_general(own, keys, LAST, preferred_element_type=F32) + bias
        weight = jax.nn.sigmoid(logits)
        if half == OWN:
            row = lax.broadcasted_iota(jnp.int32, weight.shape, 0)
            col = lax.broadcasted_iota(jnp.int32, weight.shape, 1)
            grain = row // GRAIN
            match = (grain - first) * (8 * GRAIN) + mine * GRAIN + (row - grain * GRAIN)
            on = (col == match) & (grain >= first) & (grain < first + count)
            weight = weight - jnp.where(on, 1.0, 0.0)
        weight = weight.astype(BF16)
        acc[arr] += scale * jnp.dot(weight, keys, preferred_element_type=F32)

    crossing = [(arr, k) for arr in (TXT, IMG) for k in range(COUNT)]

    def arrive(i):
        z_copy(*crossing[i]).wait_recv()
        if i + WINDOW < len(crossing):
            go(z_copy(*crossing[i + WINDOW]))
        spread_own(crossing[i][0], FAR, crossing[i][1])

    def rows_of(who, j):
        return pl.ds(pl.multiple_of(who * 576 + j * BLOCK_ROWS, 16), BLOCK_ROWS)

    def half_copy(j):
        return remote(theirs.at[j], s_buf.at[j], c_send.at[j], c_recv.at[j], sibling)

    def product(who, j):
        return jnp.dot(normed_t[rows_of(who, j)], back_ref[...], preferred_element_type=F32) * (1.0 / PAIRS)

    def image_back():
        img_back = acc[TXT]
        img_dir = img_dir_ref[...]
        back_ref[...] = ((img_back - img_dir * row_sum(img_dir * img_back)) * row_ref[2][:, :1]).astype(BF16)
        for j in range(4):
            theirs[j] = product(1 - core, j).astype(BF16)
            go(half_copy(j))

    def y_rows(d):
        return pl.ds(pl.multiple_of(((y + d) % 4) * 32, 16), PIECE)

    low, high = pl.ds(0, CUT), pl.ds(CUT, REST)
    here = y_rows(0)

    def ya_copy(j, d):
        return remote(
            summed.at[j, y_rows(d), low], ya_buf.at[d - 1, j], ya_send.at[d - 1, j], ya_recv.at[d - 1, j], y_peers[d - 1]
        )

    def xb_copy(d):
        return remote(
            summed.at[(x + d) % 4, :, high], xb_buf.at[d - 1], xb_send.at[d - 1], xb_recv.at[d - 1], x_peers[d - 1]
        )

    def first_sums():
        for j in range(4):
            own = product(core, j)
            half_copy(j).wait_recv()
            summed[j] = (own + s_buf[j].astype(F32)).astype(BF16)
            for d in (2, 1, 3):
                go(ya_copy(j, d))
        for d in (2, 1, 3):
            go(xb_copy(d))

    def norm_back():
        value = lax.dot_general(back_ref[...], proj_ref[...], LAST, preferred_element_type=F32)
        xhat = xhat_ref[...]
        g_sum[0] = jnp.sum((value * xhat).reshape(ROWS // 8, 8, WIDTH), axis=0) * (1.0 / PAIRS)
        g_begin(0)
        scaled = value * gain_ref[...]
        mean = row_sum(scaled) * (1.0 / WIDTH)
        along = row_sum(scaled * xhat) * (1.0 / WIDTH)
        feature_out[...] = (row_ref[1][:, :1] * (scaled - mean - xhat * along)).astype(BF16)

    def xa_copy(d):
        return remote(ya_sum.at[(x + d) % 4], xa_buf.at[d - 1], xa_send.at[d - 1], xa_recv.at[d - 1], x_peers[d - 1])

    def yb_copy(d):
        return remote(xb_sum.at[y_rows(d)], yb_buf.at[d - 1], yb_send.at[d - 1], yb_recv.at[d - 1], y_peers[d - 1])

    def second_sums_b():
        total = summed[x, :, high].astype(F32)
        for d in (1, 2, 3):
            xb_copy(d).wait_recv()
            total = total + xb_buf[d - 1].astype(F32)
        xb_sum[...] = total.astype(BF16)
        for d in (2, 1, 3):
            go(yb_copy(d))

    def second_sums_a():
        for j in range(4):
            total = summed[j, here, low].astype(F32)
            for d in (1, 2, 3):
                ya_copy(j, d).wait_recv()
                total = total + ya_buf[d - 1, j].astype(F32)
            ya_sum[j] = total.astype(BF16)
        for d in (2, 1, 3):
            go(xa_copy(d))

    holder = core * 4 + x

    def h_copy(half, away):
        cols = low if half == 0 else high
        size = CUT if half == 0 else REST
        return remote(
            part.at[:, cols], z_buf.at[away - 1, :, pl.ds(0, size)], h_send.at[half], h_recv.at[away - 1],
            device(x, y, holder + 8 * half, core),
        )

    def away_from(half):
        return (z - holder - 8 * half + 32) % 16

    def to_holder(half):
        away = away_from(half)

        @pl.when(away != 0)
        def _():
            h_copy(half, away).start()

    def third_sums_b():
        total = xb_sum[here].astype(F32)
        for d in (1, 2, 3):
            yb_copy(d).wait_recv()
            total = total + yb_buf[d - 1].astype(F32)
        part[:, high] = total.astype(BF16)
        to_holder(1)

    def third_sums_a():
        total = ya_sum[x].astype(F32)
        for d in (1, 2, 3):
            xa_copy(d).wait_recv()
            total = total + xa_buf[d - 1].astype(F32)
        part[:, low] = total.astype(BF16)
        to_holder(0)

    is_holder = (z % 8) == holder
    on_root_core = core == (z % 8) // 4

    def cross_copy(half):
        cols = low if half == 0 else high
        return remote(gathered.at[:, cols], gathered.at[:, cols], b_send.at[0], b_recv.at[0], far)

    def row_copy(i):
        return remote(gathered, gathered, b_send.at[1 + i], b_recv.at[1], x_peers[i])

    def core_copy():
        return remote(gathered, gathered, b_send.at[4], b_recv.at[1], sibling)

    def holder_sums():
        for half in (0, 1):

            @pl.when(is_holder & (z // 8 == half))
            def _():
                size = CUT if half == 0 else REST
                cols = low if half == 0 else high
                total = part[:, cols].astype(F32)
                for away in range(1, 16):
                    h_copy(half, away).wait_recv()
                    total = total + z_buf[away - 1, :, pl.ds(0, size)].astype(F32)
                gathered[:, cols] = total.astype(BF16)
                cross_copy(half).start()

    def holder_rows():
        for half in (0, 1):

            @pl.when(is_holder & (z // 8 == half))
            def _():
                cross_copy(1 - half).wait_recv()
                cross_copy(half).wait_send()

        @pl.when(is_holder)
        def _():
            for i in (1, 0, 2):
                row_copy(i).start()
            core_copy().start()

    def spread_rows():
        @pl.when(jnp.logical_not(is_holder))
        def _():
            row_copy(0).wait_recv()

        @pl.when(on_root_core & jnp.logical_not(is_holder))
        def _():
            core_copy().start()

        grad_out[...] = gathered[...].astype(F32)

    stages = [([sibling], 0), (y_peers, 1), (x_peers, 4), (z_quad, 7), (z_near, 10)]

    def g_copies(stage):
        peers, base = stages[stage]
        return [
            remote(g_sum.at[stage], g_buf.at[base + i], g_send.at[base + i], g_recv.at[base + i], peer)
            for i, peer in enumerate(peers)
        ]

    def g_begin(stage):
        for copy in g_copies(stage):
            go(copy)

    def g_next(stage):
        total = g_sum[stage]
        for i, copy in enumerate(g_copies(stage)):
            copy.wait_recv()
            total = total + g_buf[stages[stage][1] + i]
        g_sum[stage + 1] = total
        if stage < 4:
            g_begin(stage + 1)
        else:
            gain_out[...] = jnp.sum(total, axis=0, keepdims=True)

    def text_back():
        txt_back = acc[IMG]
        txt_dir = txt_dir_ref[...]
        text_out[...] = ((txt_back - txt_dir * row_sum(txt_dir * txt_back)) * row_ref[0][:, :1]).astype(BF16)

    def text_units():
        values = text_ref[...].astype(F32)
        txt_inv = lax.rsqrt(row_sum(values * values) + 1e-6)
        txt_dir = values * txt_inv
        txt_dir_ref[...] = txt_dir
        units[TXT, OWN, :, mine] = txt_dir.astype(BF16).reshape(GRAINS, GRAIN, WIDTH)
        row_ref[0] = jnp.broadcast_to(txt_inv, (ROWS, 128))

    def image_units():
        values = feat_ref[...].astype(F32)
        centred = values - row_sum(values) * (1.0 / WIDTH)
        deviation = lax.rsqrt(row_sum(centred * centred) * (1.0 / WIDTH) + 1e-6)
        row_ref[1] = jnp.broadcast_to(deviation, (ROWS, 128))
        xhat = centred * deviation
        xhat_ref[...] = xhat
        normed_ref[...] = (xhat * gain_ref[...]).astype(BF16)
        projected = jnp.dot(normed_ref[...], proj_ref[...], preferred_element_type=F32)
        img_inv = lax.rsqrt(row_sum(projected * projected) + 1e-6)
        row_ref[2] = jnp.broadcast_to(img_inv, (ROWS, 128))
        img_dir = projected * img_inv
        img_dir_ref[...] = img_dir
        units[IMG, OWN, :, mine] = img_dir.astype(BF16).reshape(GRAINS, GRAIN, WIDTH)

    def transpose_normed():
        normed_t[...] = normed_ref[...].T

    acc[...] = jnp.zeros_like(acc)
    text_units()
    finish_barrier()
    for i in range(WINDOW):
        go(z_copy(*crossing[i]))
    for k in range(COUNT):
        spread_own(TXT, OWN, k)
    image_units()

    plan = [(9.0, transpose_normed, ())]

    def chain(arr, half, k, neighbours, last, pairs):
        plan.append((neighbours, spread_neighbours, (arr, half, k)))
        plan.append((last, spread_last, (arr, half, k)))
        plan.append((pairs, attend, (arr, half, k)))

    for k in range(COUNT):
        chain(TXT, OWN, k, *TXT_OWN[k])
        plan.append((IMG_OWN[k][0], spread_own, (IMG, OWN, k)))
        chain(IMG, OWN, k, *IMG_OWN[k][1:])
        for arr in (TXT, IMG):
            times = FAR_TIMES[arr][k]
            plan.append((times[0], arrive, (arr * COUNT + k,)))
            chain(arr, FAR, k, *times[1:])
    tail = [
        image_back, first_sums, norm_back, second_sums_b, second_sums_a, third_sums_b, third_sums_a,
        holder_sums, holder_rows, spread_rows,
    ]
    for time, work in zip(TAIL, tail):
        plan.append((time, work, ()))
    for stage in range(5):
        plan.append((GAIN_TIMES[stage], g_next, (stage,)))
    plan.append((200.0, text_back, ()))
    for _, work, args in sorted(plan, key=lambda entry: entry[0]):
        work(*args)

    for copy in started:
        copy.wait_send()
    for half in (0, 1):
        away = away_from(half)

        @pl.when(away != 0)
        def _():
            h_copy(half, away).wait_send()

    @pl.when(is_holder)
    def _():
        for i in range(3):
            row_copy(i).wait_send()

    @pl.when(on_root_core)
    def _():
        core_copy().wait_send()


def local(features, text, proj, gain, scale, bias):
    vmem = pl.BlockSpec(memory_space=pltpu.VMEM)
    smem = pl.BlockSpec(memory_space=pltpu.SMEM)
    dma = pltpu.SemaphoreType.DMA
    feature_grad, text_grad, grad, gain_gradient = pl.pallas_call(
        pair_kernel,
        out_shape=[
            jax.ShapeDtypeStruct((ROWS, WIDTH), BF16),
            jax.ShapeDtypeStruct((ROWS, WIDTH), BF16),
            jax.ShapeDtypeStruct((PIECE, WIDTH), F32),
            jax.ShapeDtypeStruct((1, WIDTH), F32),
        ],
        in_specs=[vmem] * 4 + [smem] * 2,
        out_specs=[vmem] * 4,
        scratch_shapes=[
            pltpu.VMEM((2, 2, GRAINS, 8, GRAIN, WIDTH), BF16),
            pltpu.VMEM((2, ROWS, WIDTH), F32),
            pltpu.VMEM((ROWS, WIDTH), F32),
            pltpu.VMEM((ROWS, WIDTH), BF16),
            pltpu.VMEM((WIDTH, ROWS), BF16),
            pltpu.VMEM((ROWS, WIDTH), F32),
            pltpu.VMEM((ROWS, WIDTH), F32),
            pltpu.VMEM((3, ROWS, 128), F32),
            pltpu.VMEM((ROWS, WIDTH), BF16),
            pltpu.VMEM((4, BLOCK_ROWS, WIDTH), BF16),
            pltpu.VMEM((4, BLOCK_ROWS, WIDTH), BF16),
            pltpu.VMEM((4, BLOCK_ROWS, WIDTH), BF16),
            pltpu.VMEM((3, 4, PIECE, CUT), BF16),
            pltpu.VMEM((4, PIECE, CUT), BF16),
            pltpu.VMEM((3, BLOCK_ROWS, REST), BF16),
            pltpu.VMEM((BLOCK_ROWS, REST), BF16),
            pltpu.VMEM((3, PIECE, CUT), BF16),
            pltpu.VMEM((3, PIECE, REST), BF16),
            pltpu.VMEM((PIECE, WIDTH), BF16),
            pltpu.VMEM((15, PIECE, REST), BF16),
            pltpu.VMEM((PIECE, WIDTH), BF16),
            pltpu.VMEM((6, 8, WIDTH), F32),
            pltpu.VMEM((13, 8, WIDTH), F32),
            dma((2, 2, COUNT, 4)),
            dma((2, 2, COUNT, 4)),
            dma((2, 2, COUNT, 4)),
            dma((2, 2, COUNT, 4)),
            dma((2, COUNT)),
            dma((2, COUNT)),
            dma((4,)),
            dma((4,)),
            dma((3, 4)),
            dma((3, 4)),
            dma((3,)),
            dma((3,)),
            dma((3,)),
            dma((3,)),
            dma((3,)),
            dma((3,)),
            dma((2,)),
            dma((15,)),
            dma((5,)),
            dma((2,)),
            dma((13,)),
            dma((13,)),
        ],
        compiler_params=pltpu.CompilerParams(
            collective_id=0, has_side_effects=True, vmem_limit_bytes=60 * 2**20
        ),
        name="pairs",
    )(features[:, 0, :], text[:, 0, :], proj, gain[None, :], scale, bias)
    y = lax.axis_index("rep") % 4
    proj_grad = lax.dynamic_slice_in_dim(grad, y * 4, 36, 0)
    return feature_grad[:, None, :], text_grad[:, None, :], proj_grad, gain_gradient[0]

def solution(mesh):
    return jax.shard_map(
        local,
        mesh=mesh,
        in_specs=(P("loop", "rep", None), P("loop", "rep", None), P(), P(), P(), P()),
        out_specs=(P("loop", "rep", None), P("loop", "rep", None), P("rep", None), P()),
        check_vma=False,
    )
```

```python
import functools

import jax
import jax.numpy as jnp
from jax import lax
from jax.experimental import pallas as pl
from jax.experimental.pallas import tpu as pltpu
from jax.sharding import PartitionSpec as P

MESH = pl.DeviceIdType.MESH
WIDTH = 1152
ROWS = 192
GRAIN = 16
GRAINS = ROWS // GRAIN
CHUNKS = (4, 4, 3, 1)
STARTS = (0, 4, 8, 11)
COUNT = len(CHUNKS)
PAIRS = 3072
TXT, IMG = 0, 1
OWN, FAR = 0, 1
WINDOW = 2
BLOCK_ROWS = 144
PIECE = 48
CUT = 512
REST = WIDTH - CUT
LAST = (((1,), (1,)), ((), ()))
FIRST = (((0,), (0,)), ((), ()))
F32 = jnp.float32
BF16 = jnp.bfloat16


def coordinates():
    loop = lax.axis_index("loop")
    rep = lax.axis_index("rep")
    x = (loop // 2) % 4
    core = loop % 2
    z = (loop // 8) * 8 + rep // 4
    y = rep % 4
    return x, y, z, core


def device(x, y, z, core):
    x = (x + 4) % 4
    y = (y + 4) % 4
    z = (z + 32) % 16
    return ((z // 8) * 8 + x * 2 + core, (z % 8) * 4 + y)


def remote(src, dst, send_sem, recv_sem, target):
    return pltpu.make_async_remote_copy(
        src_ref=src,
        dst_ref=dst,
        send_sem=send_sem,
        recv_sem=recv_sem,
        device_id=target,
        device_id_type=MESH,
    )


def greet(peers):
    barrier = pltpu.get_barrier_semaphore()
    for peer in peers:
        pl.semaphore_signal(barrier, 1, device_id=peer, device_id_type=MESH)
    return lambda: pl.semaphore_wait(barrier, len(peers))


def row_sum(values):
    return jnp.sum(values, axis=-1, keepdims=True)

ONWARD = (1, -1, 1, -1)
TXT_OWN = ((5.3, 10.3, 13.0), (8.7, 13.7, 16.7), (11.2, 16.2, 19.0), (12.0, 17.0, 20.0))
IMG_OWN = ((11.0, 20.0, 26.0, 30.0), (13.0, 23.0, 29.0, 33.0), (15.0, 26.0, 32.0, 36.0), (17.0, 28.0, 34.0, 39.0))
FAR_TIMES = (
    ((24.0, 30.0, 35.0, 38.0), (36.0, 40.5, 44.0, 46.5), (44.5, 48.0, 51.0, 53.5), (47.0, 49.5, 52.0, 54.0)),
    ((69.0, 74.0, 78.5, 81.0), (76.0, 80.5, 84.5, 87.5), (82.0, 85.5, 88.3, 90.0), (84.0, 87.0, 89.5, 91.0)),
)
TAIL = (55.0, 58.0, 60.0, 66.0, 67.0, 71.0, 72.0, 86.0, 89.2, 92.0)
GAIN_TIMES = (62.5, 67.5, 72.2, 90.5, 92.5)


def pair_kernel(
    feat_ref, text_ref, proj_ref, gain_ref, scale_ref, bias_ref,
    feature_out, text_out, grad_out, gain_out,
    units, acc, xhat_ref, normed_ref, normed_t, img_dir_ref, txt_dir_ref, row_ref, back_ref,
    theirs, summed, s_buf, ya_buf, ya_sum, xb_buf, xb_sum, xa_buf, yb_buf, part, z_buf, gathered, g_sum, g_buf,
    x_send, x_recv, s_send, s_recv, z_send, z_recv,
    c_send, c_recv, ya_send, ya_recv, xb_send, xb_recv, xa_send, xa_recv, yb_send, yb_recv,
    h_send, h_recv, b_send, b_recv, g_send, g_recv,
):
    x, y, z, core = coordinates()
    mine = x * 2 + core
    sibling = device(x, y, z, 1 - core)
    plus, minus = device(x + 1, y, z, core), device(x - 1, y, z, core)
    x_peers = [plus, device(x + 2, y, z, core), minus]
    y_peers = [device(x, y + d, z, core) for d in (1, 2, 3)]
    z_peers = [device(x, y, z + d, core) for d in range(1, 16)]
    far = z_peers[7]
    finish_barrier = greet([sibling] + x_peers + y_peers + z_peers)
    scale = scale_ref[0]
    bias = bias_ref[0]
    started = []

    def go(copy):
        copy.start()
        started.append(copy)

    def slot(steps, other=0):
        owner_core = core if other == 0 else 1 - core
        return ((x + steps) % 4) * 2 + owner_core

    def block(arr, half, k, where):
        return units.at[arr, half, pl.ds(STARTS[k], CHUNKS[k]), where]

    def x_copy(arr, half, k, steps, where, target):
        ref = block(arr, half, k, where)
        return remote(ref, ref, x_send.at[arr, half, k, steps], x_recv.at[arr, half, k, steps], target)

    def s_copy(arr, half, k, steps, from_sibling=0):
        ref = block(arr, half, k, slot(steps, from_sibling))
        return remote(ref, ref, s_send.at[arr, half, k, steps], s_recv.at[arr, half, k, steps], sibling)

    def z_copy(arr, k):
        return remote(block(arr, OWN, k, mine), block(arr, FAR, k, mine), z_send.at[arr, k], z_recv.at[arr, k], far)

    def recv_x(arr, half, k, steps):
        x_copy(arr, half, k, steps, slot(steps), plus).wait_recv()

    def spread_own(arr, half, k):
        go(x_copy(arr, half, k, 3, mine, plus))
        go(x_copy(arr, half, k, 1, mine, minus))
        go(s_copy(arr, half, k, 0))

    def spread_neighbours(arr, half, k):
        recv_x(arr, half, k, 3)
        recv_x(arr, half, k, 1)
        if ONWARD[k] == 1:
            go(x_copy(arr, half, k, 2, slot(3), plus))
        else:
            go(x_copy(arr, half, k, 2, slot(1), minus))
        go(s_copy(arr, half, k, 3))
        go(s_copy(arr, half, k, 1))

    def spread_last(arr, half, k):
        recv_x(arr, half, k, 2)
        go(s_copy(arr, half, k, 2))

    def attend(arr, half, k):
        for steps in range(4):
            s_copy(arr, half, k, steps, 1).wait_recv()
        first, count = STARTS[k], CHUNKS[k]
        own = units[1 - arr, OWN, :, mine].reshape(ROWS, WIDTH)
        keys = units[arr, half, pl.ds(first, count)].reshape(count * 8 * GRAIN, WIDTH)
        logits = scale * lax.dot_general(own, keys, LAST, preferred_element_type=F32) + bias
        weight = jax.nn.sigmoid(logits)
        if half == OWN:
            row = lax.broadcasted_iota(jnp.int32, weight.shape, 0)
            col = lax.broadcasted_iota(jnp.int32, weight.shape, 1)
            grain = row // GRAIN
            match = (grain - first) * (8 * GRAIN) + mine * GRAIN + (row - grain * GRAIN)
            on = (col == match) & (grain >= first) & (grain < first + count)
            weight = weight - jnp.where(on, 1.0, 0.0)
        weight = weight.astype(BF16)
        acc[arr] += scale * jnp.dot(weight, keys, preferred_element_type=F32)

    crossing = [(arr, k) for arr in (TXT, IMG) for k in range(COUNT)]

    def arrive(i):
        z_copy(*crossing[i]).wait_recv()
        if i + WINDOW < COUNT:
            go(z_copy(*crossing[i + WINDOW]))
        if i == COUNT - 1:
            for k in range(COUNT):
                go(z_copy(IMG, k))
        spread_own(crossing[i][0], FAR, crossing[i][1])

    def rows_of(who, j):
        return pl.ds(pl.multiple_of(who * 576 + j * BLOCK_ROWS, 16), BLOCK_ROWS)

    def half_copy(j):
        return remote(theirs.at[j], s_buf.at[j], c_send.at[j], c_recv.at[j], sibling)

    def product(who, j):
        return jnp.dot(normed_t[rows_of(who, j)], back_ref[...], preferred_element_type=F32) * (1.0 / PAIRS)

    def image_back():
        img_back = acc[TXT]
        img_dir = img_dir_ref[...]
        back_ref[...] = ((img_back - img_dir * row_sum(img_dir * img_back)) * row_ref[2][:, :1]).astype(BF16)
        for j in range(4):
            theirs[j] = product(1 - core, j).astype(BF16)
            go(half_copy(j))

    def y_rows(d):
        return pl.ds(pl.multiple_of(((y + d) % 4) * 32, 16), PIECE)

    low, high = pl.ds(0, CUT), pl.ds(CUT, REST)
    here = y_rows(0)

    def ya_copy(j, d):
        return remote(
            summed.at[j, y_rows(d), low], ya_buf.at[d - 1, j], ya_send.at[d - 1, j], ya_recv.at[d - 1, j], y_peers[d - 1]
        )

    def xb_copy(d):
        return remote(
            summed.at[(x + d) % 4, :, high], xb_buf.at[d - 1], xb_send.at[d - 1], xb_recv.at[d - 1], x_peers[d - 1]
        )

    def first_sums():
        for j in range(4):
            own = product(core, j)
            half_copy(j).wait_recv()
            summed[j] = (own + s_buf[j].astype(F32)).astype(BF16)
            for d in (2, 1, 3):
                go(ya_copy(j, d))
        for d in (2, 1, 3):
            go(xb_copy(d))

    def norm_back():
        value = lax.dot_general(back_ref[...], proj_ref[...], LAST, preferred_element_type=F32)
        xhat = xhat_ref[...]
        terms = jnp.sum(value * xhat, axis=0, keepdims=True) * (1.0 / PAIRS)
        for i in range(9):
            g_sum[0, pl.ds(i, 1)] = terms[:, 128 * i : 128 * (i + 1)]
        go(g_copies(0)[0])
        scaled = value * gain_ref[...]
        mean = row_sum(scaled) * (1.0 / WIDTH)
        along = row_sum(scaled * xhat) * (1.0 / WIDTH)
        feature_out[...] = (row_ref[1][:, :1] * (scaled - mean - xhat * along)).astype(BF16)

    def xa_copy(d):
        return remote(ya_sum.at[(x + d) % 4], xa_buf.at[d - 1], xa_send.at[d - 1], xa_recv.at[d - 1], x_peers[d - 1])

    def yb_copy(d):
        return remote(xb_sum.at[y_rows(d)], yb_buf.at[d - 1], yb_send.at[d - 1], yb_recv.at[d - 1], y_peers[d - 1])

    def second_sums_b():
        total = summed[x, :, high].astype(F32)
        for d in (1, 2, 3):
            xb_copy(d).wait_recv()
            total = total + xb_buf[d - 1].astype(F32)
        xb_sum[...] = total.astype(BF16)
        for d in (2, 1, 3):
            go(yb_copy(d))

    def second_sums_a():
        for j in range(4):
            total = summed[j, here, low].astype(F32)
            for d in (1, 2, 3):
                ya_copy(j, d).wait_recv()
                total = total + ya_buf[d - 1, j].astype(F32)
            ya_sum[j] = total.astype(BF16)
        for d in (2, 1, 3):
            go(xa_copy(d))

    holder = core * 4 + x

    def h_copy(half, away):
        cols = low if half == 0 else high
        size = CUT if half == 0 else REST
        return remote(
            part.at[:, cols], z_buf.at[away - 1, :, pl.ds(0, size)], h_send.at[half], h_recv.at[away - 1],
            device(x, y, holder + 8 * half, core),
        )

    def away_from(half):
        return (z - holder - 8 * half + 32) % 16

    def to_holder(half):
        away = away_from(half)

        @pl.when(away != 0)
        def _():
            h_copy(half, away).start()

    def third_sums_b():
        total = xb_sum[here].astype(F32)
        for d in (1, 2, 3):
            yb_copy(d).wait_recv()
            total = total + yb_buf[d - 1].astype(F32)
        part[:, high] = total.astype(BF16)
        to_holder(1)

    def third_sums_a():
        total = ya_sum[x].astype(F32)
        for d in (1, 2, 3):
            xa_copy(d).wait_recv()
            total = total + xa_buf[d - 1].astype(F32)
        part[:, low] = total.astype(BF16)
        to_holder(0)

    is_holder = (z % 8) == holder
    on_root_core = core == (z % 8) // 4

    def cross_copy(half):
        cols = low if half == 0 else high
        return remote(gathered.at[:, cols], gathered.at[:, cols], b_send.at[0], b_recv.at[0], far)

    def row_copy(i):
        return remote(gathered, gathered, b_send.at[1 + i], b_recv.at[1], x_peers[i])

    def core_copy():
        return remote(gathered, gathered, b_send.at[4], b_recv.at[1], sibling)

    def holder_sums():
        for half in (0, 1):

            @pl.when(is_holder & (z // 8 == half))
            def _():
                size = CUT if half == 0 else REST
                cols = low if half == 0 else high
                total = part[:, cols].astype(F32)
                for away in range(1, 16):
                    h_copy(half, away).wait_recv()
                    total = total + z_buf[away - 1, :, pl.ds(0, size)].astype(F32)
                gathered[:, cols] = total.astype(BF16)
                cross_copy(half).start()

    def holder_rows():
        for half in (0, 1):

            @pl.when(is_holder & (z // 8 == half))
            def _():
                cross_copy(1 - half).wait_recv()
                cross_copy(half).wait_send()

        @pl.when(is_holder)
        def _():
            for i in (1, 0, 2):
                row_copy(i).start()
            core_copy().start()

    def spread_rows():
        @pl.when(jnp.logical_not(is_holder))
        def _():
            row_copy(0).wait_recv()

        @pl.when(on_root_core & jnp.logical_not(is_holder))
        def _():
            core_copy().start()

        grad_out[...] = gathered[...].astype(F32)

    stages = [([sibling], 0), (y_peers, 1), (x_peers, 4), (z_peers, 7)]

    def g_copies(stage):
        peers, base = stages[stage]
        return [
            remote(g_sum.at[stage], g_buf.at[base + i], g_send.at[base + i], g_recv.at[base + i], peer)
            for i, peer in enumerate(peers)
        ]

    def g_total(stage):
        total = g_sum[stage]
        for i, copy in enumerate(g_copies(stage)):
            copy.wait_recv()
            total = total + g_buf[stages[stage][1] + i]
        g_sum[stage + 1] = total

    def g_next(stage):
        g_total(stage)
        if stage < 2:
            for copy in g_copies(stage + 1):
                go(copy)
        else:

            @pl.when(core == 0)
            def _():
                for copy in g_copies(3):
                    copy.start()

    def g_core_copy():
        return remote(g_sum.at[4], g_sum.at[4], g_send.at[22], g_recv.at[22], sibling)

    def g_along_z():
        @pl.when(core == 0)
        def _():
            g_total(3)
            g_core_copy().start()

    def g_finish():
        @pl.when(core == 1)
        def _():
            g_core_copy().wait_recv()

        for i in range(9):
            gain_out[:, pl.ds(128 * i, 128)] = g_sum[4, pl.ds(i, 1)]

    def text_back():
        txt_back = acc[IMG]
        txt_dir = txt_dir_ref[...]
        text_out[...] = ((txt_back - txt_dir * row_sum(txt_dir * txt_back)) * row_ref[0][:, :1]).astype(BF16)

    def text_units():
        values = text_ref[...].astype(F32)
        txt_inv = lax.rsqrt(row_sum(values * values) + 1e-6)
        txt_dir = values * txt_inv
        txt_dir_ref[...] = txt_dir
        units[TXT, OWN, :, mine] = txt_dir.astype(BF16).reshape(GRAINS, GRAIN, WIDTH)
        row_ref[0] = jnp.broadcast_to(txt_inv, (ROWS, 128))

    def image_units():
        values = feat_ref[...].astype(F32)
        centred = values - row_sum(values) * (1.0 / WIDTH)
        deviation = lax.rsqrt(row_sum(centred * centred) * (1.0 / WIDTH) + 1e-6)
        row_ref[1] = jnp.broadcast_to(deviation, (ROWS, 128))
        xhat = centred * deviation
        xhat_ref[...] = xhat
        normed_ref[...] = (xhat * gain_ref[...]).astype(BF16)
        projected = jnp.dot(normed_ref[...], proj_ref[...], preferred_element_type=F32)
        img_inv = lax.rsqrt(row_sum(projected * projected) + 1e-6)
        row_ref[2] = jnp.broadcast_to(img_inv, (ROWS, 128))
        img_dir = projected * img_inv
        img_dir_ref[...] = img_dir
        units[IMG, OWN, :, mine] = img_dir.astype(BF16).reshape(GRAINS, GRAIN, WIDTH)

    def transpose_normed():
        normed_t[...] = normed_ref[...].T

    acc[...] = jnp.zeros_like(acc)
    text_units()
    finish_barrier()
    for i in range(WINDOW):
        go(z_copy(*crossing[i]))
    for k in range(COUNT):
        spread_own(TXT, OWN, k)
    image_units()

    plan = [(9.0, transpose_normed, ())]

    def chain(arr, half, k, neighbours, last, pairs):
        plan.append((neighbours, spread_neighbours, (arr, half, k)))
        plan.append((last, spread_last, (arr, half, k)))
        plan.append((pairs, attend, (arr, half, k)))

    for k in range(COUNT):
        chain(TXT, OWN, k, *TXT_OWN[k])
        plan.append((IMG_OWN[k][0], spread_own, (IMG, OWN, k)))
        chain(IMG, OWN, k, *IMG_OWN[k][1:])
        for arr in (TXT, IMG):
            times = FAR_TIMES[arr][k]
            plan.append((times[0], arrive, (arr * COUNT + k,)))
            chain(arr, FAR, k, *times[1:])
    tail = [
        image_back, first_sums, norm_back, second_sums_b, second_sums_a, third_sums_b, third_sums_a,
        holder_sums, holder_rows, spread_rows,
    ]
    for time, work in zip(TAIL, tail):
        plan.append((time, work, ()))
    for stage in range(3):
        plan.append((GAIN_TIMES[stage], g_next, (stage,)))
    plan.append((GAIN_TIMES[3], g_along_z, ()))
    plan.append((GAIN_TIMES[4], g_finish, ()))
    plan.append((200.0, text_back, ()))
    for _, work, args in sorted(plan, key=lambda entry: entry[0]):
        work(*args)

    for copy in started:
        copy.wait_send()
    for half in (0, 1):
        away = away_from(half)

        @pl.when(away != 0)
        def _():
            h_copy(half, away).wait_send()

    @pl.when(is_holder)
    def _():
        for i in range(3):
            row_copy(i).wait_send()

    @pl.when(on_root_core)
    def _():
        core_copy().wait_send()

    @pl.when(core == 0)
    def _():
        for copy in g_copies(3):
            copy.wait_send()
        g_core_copy().wait_send()


def local(features, text, proj, gain, scale, bias):
    vmem = pl.BlockSpec(memory_space=pltpu.VMEM)
    smem = pl.BlockSpec(memory_space=pltpu.SMEM)
    dma = pltpu.SemaphoreType.DMA
    feature_grad, text_grad, grad, gain_gradient = pl.pallas_call(
        pair_kernel,
        out_shape=[
            jax.ShapeDtypeStruct((ROWS, WIDTH), BF16),
            jax.ShapeDtypeStruct((ROWS, WIDTH), BF16),
            jax.ShapeDtypeStruct((PIECE, WIDTH), F32),
            jax.ShapeDtypeStruct((1, WIDTH), F32),
        ],
        in_specs=[vmem] * 4 + [smem] * 2,
        out_specs=[vmem] * 4,
        scratch_shapes=[
            pltpu.VMEM((2, 2, GRAINS, 8, GRAIN, WIDTH), BF16),
            pltpu.VMEM((2, ROWS, WIDTH), F32),
            pltpu.VMEM((ROWS, WIDTH), F32),
            pltpu.VMEM((ROWS, WIDTH), BF16),
            pltpu.VMEM((WIDTH, ROWS), BF16),
            pltpu.VMEM((ROWS, WIDTH), F32),
            pltpu.VMEM((ROWS, WIDTH), F32),
            pltpu.VMEM((3, ROWS, 128), F32),
            pltpu.VMEM((ROWS, WIDTH), BF16),
            pltpu.VMEM((4, BLOCK_ROWS, WIDTH), BF16),
            pltpu.VMEM((4, BLOCK_ROWS, WIDTH), BF16),
            pltpu.VMEM((4, BLOCK_ROWS, WIDTH), BF16),
            pltpu.VMEM((3, 4, PIECE, CUT), BF16),
            pltpu.VMEM((4, PIECE, CUT), BF16),
            pltpu.VMEM((3, BLOCK_ROWS, REST), BF16),
            pltpu.VMEM((BLOCK_ROWS, REST), BF16),
            pltpu.VMEM((3, PIECE, CUT), BF16),
            pltpu.VMEM((3, PIECE, REST), BF16),
            pltpu.VMEM((PIECE, WIDTH), BF16),
            pltpu.VMEM((15, PIECE, REST), BF16),
            pltpu.VMEM((PIECE, WIDTH), BF16),
            pltpu.VMEM((5, 9, 128), F32),
            pltpu.VMEM((22, 9, 128), F32),
            dma((2, 2, COUNT, 4)),
            dma((2, 2, COUNT, 4)),
            dma((2, 2, COUNT, 4)),
            dma((2, 2, COUNT, 4)),
            dma((2, COUNT)),
            dma((2, COUNT)),
            dma((4,)),
            dma((4,)),
            dma((3, 4)),
            dma((3, 4)),
            dma((3,)),
            dma((3,)),
            dma((3,)),
            dma((3,)),
            dma((3,)),
            dma((3,)),
            dma((2,)),
            dma((15,)),
            dma((5,)),
            dma((2,)),
            dma((23,)),
            dma((23,)),
        ],
        compiler_params=pltpu.CompilerParams(
            collective_id=0, has_side_effects=True, vmem_limit_bytes=60 * 2**20
        ),
        name="pairs",
    )(features[:, 0, :], text[:, 0, :], proj, gain[None, :], scale, bias)
    y = lax.axis_index("rep") % 4
    proj_grad = lax.dynamic_slice_in_dim(grad, y * 4, 36, 0)
    return feature_grad[:, None, :], text_grad[:, None, :], proj_grad, gain_gradient[0]

def solution(mesh):
    return jax.shard_map(
        local,
        mesh=mesh,
        in_specs=(P("loop", "rep", None), P("loop", "rep", None), P(), P(), P(), P()),
        out_specs=(P("loop", "rep", None), P("loop", "rep", None), P("rep", None), P()),
        check_vma=False,
    )
```

```python
import functools

import jax
import jax.numpy as jnp
from jax import lax
from jax.experimental import pallas as pl
from jax.experimental.pallas import tpu as pltpu
from jax.sharding import PartitionSpec as P

MESH = pl.DeviceIdType.MESH
WIDTH = 1152
ROWS = 192
GRAIN = 16
GRAINS = ROWS // GRAIN
CHUNKS = ((6, 6), (4, 4, 3, 1))
STARTS = ((0, 6), (0, 4, 8, 11))
OWN_COUNT, COUNT = len(CHUNKS[0]), len(CHUNKS[1])
PAIRS = 3072
TXT, IMG = 0, 1
OWN, FAR = 0, 1
IMAGES_AFTER = 1
BLOCK_ROWS = 144
PIECE = 48
CUT = 512
REST = WIDTH - CUT
LAST = (((1,), (1,)), ((), ()))
FIRST = (((0,), (0,)), ((), ()))
F32 = jnp.float32
BF16 = jnp.bfloat16


def coordinates():
    loop = lax.axis_index("loop")
    rep = lax.axis_index("rep")
    x = (loop // 2) % 4
    core = loop % 2
    z = (loop // 8) * 8 + rep // 4
    y = rep % 4
    return x, y, z, core


def device(x, y, z, core):
    x = (x + 4) % 4
    y = (y + 4) % 4
    z = (z + 32) % 16
    return ((z // 8) * 8 + x * 2 + core, (z % 8) * 4 + y)


def remote(src, dst, send_sem, recv_sem, target):
    return pltpu.make_async_remote_copy(
        src_ref=src,
        dst_ref=dst,
        send_sem=send_sem,
        recv_sem=recv_sem,
        device_id=target,
        device_id_type=MESH,
    )


def greet(peers):
    barrier = pltpu.get_barrier_semaphore()
    for peer in peers:
        pl.semaphore_signal(barrier, 1, device_id=peer, device_id_type=MESH)
    return lambda: pl.semaphore_wait(barrier, len(peers))


def row_sum(values):
    return jnp.sum(values, axis=-1, keepdims=True)

ONWARD = ((1, -1), (1, -1, 1, -1))
TXT_OWN = ((6.0, 22.0, 27.1), (11.0, 23.0, 33.0))
IMG_OWN = ((16.0, 58.5, 63.1), (21.0, 58.6, 64.1))
FAR_TIMES = (
    ((27.0, 32.5, 36.0, 39.0), (34.0, 38.5, 42.5, 43.5), (38.6, 46.5, 49.0, 51.0), (42.6, 47.5, 50.0, 52.0)),
    ((61.0, 68.0, 74.5, 80.6), (67.6, 73.0, 78.5, 87.5), (74.0, 80.5, 86.8, 90.0), (80.0, 86.5, 89.0, 91.0)),
)
DRAINS = ((63.0, 0.6), (78.6, 0.8))
TAIL = (53.0, 58.0, 60.0, 66.0, 67.0, 71.0, 72.0, 81.2, 86.0, 92.0)
GAIN_TIMES = (62.5, 67.5, 72.2, 90.5, 92.5)


def pair_kernel(
    feat_ref, text_ref, proj_ref, gain_ref, scale_ref, bias_ref,
    feature_out, text_out, grad_out, gain_out,
    units, acc, xhat_ref, normed_ref, normed_t, img_dir_ref, txt_dir_ref, row_ref, back_ref,
    theirs, summed, s_buf, ya_buf, ya_sum, xb_buf, xb_sum, xa_buf, yb_buf, part, z_buf, gathered, g_sum, g_buf,
    x_send, x_recv, s_send, s_recv, z_send, z_recv,
    c_send, c_recv, ya_send, ya_recv, xb_send, xb_recv, xa_send, xa_recv, yb_send, yb_recv,
    h_send, h_recv, b_send, b_recv, g_send, g_recv,
):
    x, y, z, core = coordinates()
    mine = x * 2 + core
    sibling = device(x, y, z, 1 - core)
    plus, minus = device(x + 1, y, z, core), device(x - 1, y, z, core)
    x_peers = [plus, device(x + 2, y, z, core), minus]
    y_peers = [device(x, y + d, z, core) for d in (1, 2, 3)]
    z_peers = [device(x, y, z + d, core) for d in range(1, 16)]
    far = z_peers[7]
    finish_barrier = greet([sibling] + x_peers + y_peers + z_peers)
    scale = scale_ref[0]
    bias = bias_ref[0]
    started = []

    def go(copy):
        copy.start()
        started.append(copy)

    def slot(steps, other=0):
        owner_core = core if other == 0 else 1 - core
        return ((x + steps) % 4) * 2 + owner_core

    def block(arr, half, k, where):
        return units.at[arr, half, pl.ds(STARTS[half][k], CHUNKS[half][k]), where]

    def x_copy(arr, half, k, steps, where, target):
        ref = block(arr, half, k, where)
        return remote(ref, ref, x_send.at[arr, half, k, steps], x_recv.at[arr, half, k, steps], target)

    def s_copy(arr, half, k, steps, from_sibling=0):
        ref = block(arr, half, k, slot(steps, from_sibling))
        return remote(ref, ref, s_send.at[arr, half, k, steps], s_recv.at[arr, half, k, steps], sibling)

    def z_copy(arr, k):
        src = units.at[arr, OWN, pl.ds(STARTS[FAR][k], CHUNKS[FAR][k]), mine]
        return remote(src, block(arr, FAR, k, mine), z_send.at[arr, k], z_recv.at[arr, k], far)

    def recv_x(arr, half, k, steps):
        x_copy(arr, half, k, steps, slot(steps), plus).wait_recv()

    def spread_own(arr, half, k):
        go(x_copy(arr, half, k, 3, mine, plus))
        go(x_copy(arr, half, k, 1, mine, minus))
        go(s_copy(arr, half, k, 0))

    def spread_neighbours(arr, half, k):
        recv_x(arr, half, k, 3)
        recv_x(arr, half, k, 1)
        if ONWARD[half][k] == 1:
            go(x_copy(arr, half, k, 2, slot(3), plus))
        else:
            go(x_copy(arr, half, k, 2, slot(1), minus))
        go(s_copy(arr, half, k, 3))
        go(s_copy(arr, half, k, 1))

    def spread_last(arr, half, k):
        recv_x(arr, half, k, 2)
        go(s_copy(arr, half, k, 2))

    def attend(arr, half, k):
        for steps in range(4):
            s_copy(arr, half, k, steps, 1).wait_recv()
        first, count = STARTS[half][k], CHUNKS[half][k]
        own = units[1 - arr, OWN, :, mine].reshape(ROWS, WIDTH)
        keys = units[arr, half, pl.ds(first, count)].reshape(count * 8 * GRAIN, WIDTH)
        logits = scale * lax.dot_general(own, keys, LAST, preferred_element_type=F32) + bias
        weight = jax.nn.sigmoid(logits)
        if half == OWN:
            row = lax.broadcasted_iota(jnp.int32, weight.shape, 0)
            col = lax.broadcasted_iota(jnp.int32, weight.shape, 1)
            grain = row // GRAIN
            match = (grain - first) * (8 * GRAIN) + mine * GRAIN + (row - grain * GRAIN)
            on = (col == match) & (grain >= first) & (grain < first + count)
            weight = weight - jnp.where(on, 1.0, 0.0)
        weight = weight.astype(BF16)
        acc[arr] += scale * jnp.dot(weight, keys, preferred_element_type=F32)

    crossing = [(arr, k) for arr in (TXT, IMG) for k in range(COUNT)]

    def arrive(i):
        z_copy(*crossing[i]).wait_recv()
        if i == IMAGES_AFTER:
            for k in range(COUNT):
                go(z_copy(IMG, k))
        spread_own(crossing[i][0], FAR, crossing[i][1])

    def rows_of(who, j):
        return pl.ds(pl.multiple_of(who * 576 + j * BLOCK_ROWS, 16), BLOCK_ROWS)

    def half_copy(j):
        return remote(theirs.at[j], s_buf.at[j], c_send.at[j], c_recv.at[j], sibling)

    def product(who, j):
        return jnp.dot(normed_t[rows_of(who, j)], back_ref[...], preferred_element_type=F32) * (1.0 / PAIRS)

    def image_back():
        img_back = acc[TXT]
        img_dir = img_dir_ref[...]
        back_ref[...] = ((img_back - img_dir * row_sum(img_dir * img_back)) * row_ref[2][:, :1]).astype(BF16)
        for j in range(4):
            theirs[j] = product(1 - core, j).astype(BF16)
            go(half_copy(j))

    def y_rows(d):
        return pl.ds(pl.multiple_of(((y + d) % 4) * 32, 16), PIECE)

    low, high = pl.ds(0, CUT), pl.ds(CUT, REST)
    here = y_rows(0)

    def ya_copy(d):
        return remote(
            summed.at[:, y_rows(d), low], ya_buf.at[d - 1], ya_send.at[d - 1], ya_recv.at[d - 1], y_peers[d - 1]
        )

    def xb_copy(d):
        return remote(
            summed.at[(x + d) % 4, :, high], xb_buf.at[d - 1], xb_send.at[d - 1], xb_recv.at[d - 1], x_peers[d - 1]
        )

    def first_sums():
        for j in range(4):
            own = product(core, j)
            half_copy(j).wait_recv()
            summed[j] = (own + s_buf[j].astype(F32)).astype(BF16)
        for d in (2, 1, 3):
            go(ya_copy(d))
            go(xb_copy(d))

    def norm_back():
        value = lax.dot_general(back_ref[...], proj_ref[...], LAST, preferred_element_type=F32)
        xhat = xhat_ref[...]
        terms = jnp.sum(value * xhat, axis=0, keepdims=True) * (1.0 / PAIRS)
        for i in range(9):
            g_sum[0, pl.ds(i, 1)] = terms[:, 128 * i : 128 * (i + 1)]
        go(g_copies(0)[0])
        scaled = value * gain_ref[...].reshape(1, WIDTH)
        mean = row_sum(scaled) * (1.0 / WIDTH)
        along = row_sum(scaled * xhat) * (1.0 / WIDTH)
        feature_out[...] = (row_ref[1][:, :1] * (scaled - mean - xhat * along)).astype(BF16)

    def xa_copy(d):
        return remote(ya_sum.at[(x + d) % 4], xa_buf.at[d - 1], xa_send.at[d - 1], xa_recv.at[d - 1], x_peers[d - 1])

    def yb_copy(d):
        return remote(xb_sum.at[y_rows(d)], yb_buf.at[d - 1], yb_send.at[d - 1], yb_recv.at[d - 1], y_peers[d - 1])

    def second_sums_b():
        total = summed[x, :, high].astype(F32)
        for d in (1, 2, 3):
            xb_copy(d).wait_recv()
            total = total + xb_buf[d - 1].astype(F32)
        xb_sum[...] = total.astype(BF16)
        for d in (2, 1, 3):
            go(yb_copy(d))

    def second_sums_a():
        for d in (1, 2, 3):
            ya_copy(d).wait_recv()
        for j in range(4):
            total = summed[j, here, low].astype(F32)
            for d in (1, 2, 3):
                total = total + ya_buf[d - 1, j].astype(F32)
            ya_sum[j] = total.astype(BF16)
        for d in (2, 1, 3):
            go(xa_copy(d))

    holder = core * 4 + x

    def h_copy(half, away):
        cols = low if half == 0 else high
        size = CUT if half == 0 else REST
        return remote(
            part.at[:, cols], z_buf.at[away - 1, :, pl.ds(0, size)], h_send.at[half], h_recv.at[away - 1],
            device(x, y, holder + 8 * half, core),
        )

    def away_from(half):
        return (z - holder - 8 * half + 32) % 16

    def to_holder(half):
        away = away_from(half)

        @pl.when(away != 0)
        def _():
            h_copy(half, away).start()

    def third_sums_b():
        total = xb_sum[here].astype(F32)
        for d in (1, 2, 3):
            yb_copy(d).wait_recv()
            total = total + yb_buf[d - 1].astype(F32)
        part[:, high] = total.astype(BF16)
        to_holder(1)

    def third_sums_a():
        total = ya_sum[x].astype(F32)
        for d in (1, 2, 3):
            xa_copy(d).wait_recv()
            total = total + xa_buf[d - 1].astype(F32)
        part[:, low] = total.astype(BF16)
        to_holder(0)

    is_holder = (z % 8) == holder
    on_root_core = core == (z % 8) // 4

    def cross_copy(half):
        cols = low if half == 0 else high
        return remote(gathered.at[:, cols], gathered.at[:, cols], b_send.at[0], b_recv.at[0], far)

    def row_copy(i):
        return remote(gathered, gathered, b_send.at[1 + i], b_recv.at[1], x_peers[i])

    def core_copy():
        return remote(gathered, gathered, b_send.at[4], b_recv.at[1], sibling)

    def holder_sums():
        for half in (0, 1):

            @pl.when(is_holder & (z // 8 == half))
            def _():
                size = CUT if half == 0 else REST
                cols = low if half == 0 else high
                total = part[:, cols].astype(F32)
                for away in range(1, 16):
                    h_copy(half, away).wait_recv()
                    total = total + z_buf[away - 1, :, pl.ds(0, size)].astype(F32)
                gathered[:, cols] = total.astype(BF16)
                cross_copy(half).start()

    def holder_rows():
        for half in (0, 1):

            @pl.when(is_holder & (z // 8 == half))
            def _():
                cross_copy(1 - half).wait_recv()
                cross_copy(half).wait_send()

        @pl.when(is_holder)
        def _():
            for i in (1, 0, 2):
                row_copy(i).start()
            core_copy().start()

    def spread_rows():
        @pl.when(jnp.logical_not(is_holder))
        def _():
            row_copy(0).wait_recv()

        @pl.when(on_root_core & jnp.logical_not(is_holder))
        def _():
            core_copy().start()

        for p in range(4):

            @pl.when(y == p)
            def _():
                grad_out[...] = gathered[...].astype(F32)[4 * p : 4 * p + WIDTH // 32]

    stages = [([sibling], 0), (y_peers, 1), (x_peers, 4), (z_peers, 7)]

    def g_copies(stage):
        peers, base = stages[stage]
        return [
            remote(g_sum.at[stage], g_buf.at[base + i], g_send.at[base + i], g_recv.at[base + i], peer)
            for i, peer in enumerate(peers)
        ]

    def g_total(stage):
        total = g_sum[stage]
        for i, copy in enumerate(g_copies(stage)):
            copy.wait_recv()
            total = total + g_buf[stages[stage][1] + i]
        g_sum[stage + 1] = total

    def g_next(stage):
        g_total(stage)
        if stage < 2:
            for copy in g_copies(stage + 1):
                go(copy)
        else:

            @pl.when(core == 0)
            def _():
                for copy in g_copies(3):
                    copy.start()

    def g_core_copy():
        return remote(g_sum.at[4], g_sum.at[4], g_send.at[22], g_recv.at[22], sibling)

    def g_along_z():
        @pl.when(core == 0)
        def _():
            g_total(3)
            g_core_copy().start()

    def g_finish():
        @pl.when(core == 1)
        def _():
            g_core_copy().wait_recv()

        for i in range(9):
            gain_out[pl.ds(128 * i, 128)] = g_sum[4, i]

    def text_back():
        txt_back = acc[IMG]
        txt_dir = txt_dir_ref[...]
        text_out[...] = ((txt_back - txt_dir * row_sum(txt_dir * txt_back)) * row_ref[0][:, :1]).astype(BF16)

    def text_units():
        values = text_ref[...].astype(F32)
        txt_inv = lax.rsqrt(row_sum(values * values) + 1e-6)
        txt_dir = values * txt_inv
        txt_dir_ref[...] = txt_dir
        units[TXT, OWN, :, mine] = txt_dir.astype(BF16).reshape(GRAINS, GRAIN, WIDTH)
        row_ref[0] = jnp.broadcast_to(txt_inv, (ROWS, 128))

    def image_units():
        values = feat_ref[...].astype(F32)
        centred = values - row_sum(values) * (1.0 / WIDTH)
        deviation = lax.rsqrt(row_sum(centred * centred) * (1.0 / WIDTH) + 1e-6)
        row_ref[1] = jnp.broadcast_to(deviation, (ROWS, 128))
        xhat = centred * deviation
        xhat_ref[...] = xhat
        normed_ref[...] = (xhat * gain_ref[...].reshape(1, WIDTH)).astype(BF16)
        projected = jnp.dot(normed_ref[...], proj_ref[...], preferred_element_type=F32)
        img_inv = lax.rsqrt(row_sum(projected * projected) + 1e-6)
        row_ref[2] = jnp.broadcast_to(img_inv, (ROWS, 128))
        img_dir = projected * img_inv
        img_dir_ref[...] = img_dir
        units[IMG, OWN, :, mine] = img_dir.astype(BF16).reshape(GRAINS, GRAIN, WIDTH)

    def transpose_normed():
        normed_t[...] = normed_ref[...].T

    acc[...] = jnp.zeros_like(acc)
    text_units()
    finish_barrier()
    for k in range(COUNT):
        go(z_copy(TXT, k))
    for k in range(OWN_COUNT):
        spread_own(TXT, OWN, k)
    image_units()
    for k in range(OWN_COUNT):
        spread_own(IMG, OWN, k)

    plan = [(5.0, transpose_normed, ())]

    def chain(arr, half, k, neighbours, last, pairs):
        plan.append((neighbours, spread_neighbours, (arr, half, k)))
        plan.append((last, spread_last, (arr, half, k)))
        plan.append((pairs, attend, (arr, half, k)))

    for k in range(OWN_COUNT):
        chain(TXT, OWN, k, *TXT_OWN[k])
        chain(IMG, OWN, k, *IMG_OWN[k])
    for k in range(COUNT):
        for arr in (TXT, IMG):
            times = FAR_TIMES[arr][k]
            plan.append((times[0], arrive, (arr * COUNT + k,)))
            chain(arr, FAR, k, *times[1:])
    tail = [
        image_back, first_sums, norm_back, second_sums_b, second_sums_a, third_sums_b, third_sums_a,
        holder_sums, holder_rows, spread_rows,
    ]
    for time, work in zip(TAIL, tail):
        plan.append((time, work, ()))
    for stage in range(3):
        plan.append((GAIN_TIMES[stage], g_next, (stage,)))
    plan.append((GAIN_TIMES[3], g_along_z, ()))
    plan.append((GAIN_TIMES[4], g_finish, ()))
    plan.append((200.0, text_back, ()))

    def drain(fraction):
        for _ in range(int(len(started) * fraction)):
            started.pop(0).wait_send()

    for time, fraction in DRAINS:
        plan.append((time, drain, (fraction,)))
    for _, work, args in sorted(plan, key=lambda entry: entry[0]):
        work(*args)

    drain(1.0)
    for half in (0, 1):
        away = away_from(half)

        @pl.when(away != 0)
        def _():
            h_copy(half, away).wait_send()

    @pl.when(is_holder)
    def _():
        for i in range(3):
            row_copy(i).wait_send()

    @pl.when(on_root_core)
    def _():
        core_copy().wait_send()

    @pl.when(core == 0)
    def _():
        for copy in g_copies(3):
            copy.wait_send()
        g_core_copy().wait_send()


def local(features, text, proj, gain, scale, bias):
    vmem = pl.BlockSpec(memory_space=pltpu.VMEM)
    smem = pl.BlockSpec(memory_space=pltpu.SMEM)
    dma = pltpu.SemaphoreType.DMA
    feature_grad, text_grad, grad, gain_gradient = pl.pallas_call(
        pair_kernel,
        out_shape=[
            jax.ShapeDtypeStruct((ROWS, WIDTH), BF16),
            jax.ShapeDtypeStruct((ROWS, WIDTH), BF16),
            jax.ShapeDtypeStruct((WIDTH // 32, WIDTH), F32),
            jax.ShapeDtypeStruct((WIDTH,), F32),
        ],
        in_specs=[vmem] * 4 + [smem] * 2,
        out_specs=[vmem] * 4,
        scratch_shapes=[
            pltpu.VMEM((2, 2, GRAINS, 8, GRAIN, WIDTH), BF16),
            pltpu.VMEM((2, ROWS, WIDTH), F32),
            pltpu.VMEM((ROWS, WIDTH), F32),
            pltpu.VMEM((ROWS, WIDTH), BF16),
            pltpu.VMEM((WIDTH, ROWS), BF16),
            pltpu.VMEM((ROWS, WIDTH), F32),
            pltpu.VMEM((ROWS, WIDTH), F32),
            pltpu.VMEM((3, ROWS, 128), F32),
            pltpu.VMEM((ROWS, WIDTH), BF16),
            pltpu.VMEM((4, BLOCK_ROWS, WIDTH), BF16),
            pltpu.VMEM((4, BLOCK_ROWS, WIDTH), BF16),
            pltpu.VMEM((4, BLOCK_ROWS, WIDTH), BF16),
            pltpu.VMEM((3, 4, PIECE, CUT), BF16),
            pltpu.VMEM((4, PIECE, CUT), BF16),
            pltpu.VMEM((3, BLOCK_ROWS, REST), BF16),
            pltpu.VMEM((BLOCK_ROWS, REST), BF16),
            pltpu.VMEM((3, PIECE, CUT), BF16),
            pltpu.VMEM((3, PIECE, REST), BF16),
            pltpu.VMEM((PIECE, WIDTH), BF16),
            pltpu.VMEM((15, PIECE, REST), BF16),
            pltpu.VMEM((PIECE, WIDTH), BF16),
            pltpu.VMEM((5, 9, 128), F32),
            pltpu.VMEM((22, 9, 128), F32),
            dma((2, 2, COUNT, 4)),
            dma((2, 2, COUNT, 4)),
            dma((2, 2, COUNT, 4)),
            dma((2, 2, COUNT, 4)),
            dma((2, COUNT)),
            dma((2, COUNT)),
            dma((4,)),
            dma((4,)),
            dma((3,)),
            dma((3,)),
            dma((3,)),
            dma((3,)),
            dma((3,)),
            dma((3,)),
            dma((3,)),
            dma((3,)),
            dma((2,)),
            dma((15,)),
            dma((5,)),
            dma((2,)),
            dma((23,)),
            dma((23,)),
        ],
        compiler_params=pltpu.CompilerParams(
            collective_id=0, has_side_effects=True, vmem_limit_bytes=60 * 2**20
        ),
        name="pairs",
    )(features[:, 0, :], text[:, 0, :], proj, gain, scale, bias)
    return feature_grad[:, None, :], text_grad[:, None, :], grad, gain_gradient

def solution(mesh):
    return jax.shard_map(
        local,
        mesh=mesh,
        in_specs=(P("loop", "rep", None), P("loop", "rep", None), P(), P(), P(), P()),
        out_specs=(P("loop", "rep", None), P("loop", "rep", None), P("rep", None), P()),
        check_vma=False,
    )
```

```python
import functools

import jax
import jax.numpy as jnp
from jax import lax
from jax.experimental import pallas as pl
from jax.experimental.pallas import tpu as pltpu
from jax.sharding import PartitionSpec as P

MESH = pl.DeviceIdType.MESH
WIDTH = 1152
ROWS = 192
GRAIN = 16
GRAINS = ROWS // GRAIN
CHUNKS = ((6, 6), (5, 5, 2))
STARTS = ((0, 6), (0, 5, 10))
OWN_COUNT, COUNT = len(CHUNKS[0]), len(CHUNKS[1])
PAIRS = 3072
TXT, IMG = 0, 1
OWN, FAR = 0, 1
IMAGES_AFTER = 1
BLOCK_ROWS = 144
PIECE = 48
CUT = 512
REST = WIDTH - CUT
LAST = (((1,), (1,)), ((), ()))
FIRST = (((0,), (0,)), ((), ()))
F32 = jnp.float32
BF16 = jnp.bfloat16


def coordinates():
    loop = lax.axis_index("loop")
    rep = lax.axis_index("rep")
    x = (loop // 2) % 4
    core = loop % 2
    z = (loop // 8) * 8 + rep // 4
    y = rep % 4
    return x, y, z, core


def device(x, y, z, core):
    x = (x + 4) % 4
    y = (y + 4) % 4
    z = (z + 32) % 16
    return ((z // 8) * 8 + x * 2 + core, (z % 8) * 4 + y)


def remote(src, dst, send_sem, recv_sem, target):
    return pltpu.make_async_remote_copy(
        src_ref=src,
        dst_ref=dst,
        send_sem=send_sem,
        recv_sem=recv_sem,
        device_id=target,
        device_id_type=MESH,
    )


def greet(peers):
    barrier = pltpu.get_barrier_semaphore()
    for peer in peers:
        pl.semaphore_signal(barrier, 1, device_id=peer, device_id_type=MESH)
    return lambda: pl.semaphore_wait(barrier, len(peers))


def row_sum(values):
    return jnp.sum(values, axis=-1, keepdims=True)

ONWARD = ((1, -1), (1, -1, 1))
TXT_OWN = ((6.0, 22.0, 30.5), (11.0, 23.0, 33.0))
IMG_OWN = ((16.0, 61.0, 63.1), (21.0, 61.1, 64.1))
FAR_TIMES = (
    ((27.0, 32.0, 36.0, 39.5), (34.0, 39.0, 43.2, 47.5), (43.0, 46.0, 49.0, 50.0)),
    ((67.4, 72.5, 76.0, 79.5), (72.3, 77.5, 81.0, 83.5), (77.0, 80.5, 84.0, 86.0)),
)
DRAINS = ((63.0, 0.6), (78.6, 0.8))
TAIL = (53.0, 58.0, 60.0, 66.0, 67.0, 71.0, 72.0, 80.0, 83.0, 87.0)
GAIN_TIMES = (62.5, 67.5, 72.2, 86.5, 88.0)


def pair_kernel(
    feat_ref, text_ref, proj_ref, gain_ref, scale_ref, bias_ref,
    feature_out, text_out, grad_out, gain_out,
    units, acc, xhat_ref, normed_ref, normed_t, img_dir_ref, txt_dir_ref, row_ref, back_ref,
    theirs, summed, s_buf, ya_buf, ya_sum, xb_buf, xb_sum, xa_buf, yb_buf, part, z_buf, gathered, g_sum, g_buf,
    x_send, x_recv, s_send, s_recv, z_send, z_recv,
    c_send, c_recv, ya_send, ya_recv, xb_send, xb_recv, xa_send, xa_recv, yb_send, yb_recv,
    h_send, h_recv, b_send, b_recv, g_send, g_recv,
):
    x, y, z, core = coordinates()
    mine = x * 2 + core
    sibling = device(x, y, z, 1 - core)
    plus, minus = device(x + 1, y, z, core), device(x - 1, y, z, core)
    x_peers = [plus, device(x + 2, y, z, core), minus]
    y_peers = [device(x, y + d, z, core) for d in (1, 2, 3)]
    z_peers = [device(x, y, z + d, core) for d in range(1, 16)]
    far = z_peers[7]
    finish_barrier = greet([sibling] + x_peers + y_peers + z_peers)
    scale = scale_ref[0]
    bias = bias_ref[0]
    started = []

    def go(copy):
        copy.start()
        started.append(copy)

    def slot(steps, other=0):
        owner_core = core if other == 0 else 1 - core
        return ((x + steps) % 4) * 2 + owner_core

    def block(arr, half, k, where):
        return units.at[arr, half, pl.ds(STARTS[half][k], CHUNKS[half][k]), where]

    def x_copy(arr, half, k, steps, where, target):
        ref = block(arr, half, k, where)
        return remote(ref, ref, x_send.at[arr, half, k, steps], x_recv.at[arr, half, k, steps], target)

    def s_copy(arr, half, k, steps, from_sibling=0):
        ref = block(arr, half, k, slot(steps, from_sibling))
        return remote(ref, ref, s_send.at[arr, half, k, steps], s_recv.at[arr, half, k, steps], sibling)

    def z_copy(arr, k):
        src = units.at[arr, OWN, pl.ds(STARTS[FAR][k], CHUNKS[FAR][k]), mine]
        return remote(src, block(arr, FAR, k, mine), z_send.at[arr, k], z_recv.at[arr, k], far)

    def recv_x(arr, half, k, steps):
        x_copy(arr, half, k, steps, slot(steps), plus).wait_recv()

    def spread_own(arr, half, k):
        go(x_copy(arr, half, k, 3, mine, plus))
        go(x_copy(arr, half, k, 1, mine, minus))
        go(s_copy(arr, half, k, 0))

    def spread_neighbours(arr, half, k):
        recv_x(arr, half, k, 3)
        recv_x(arr, half, k, 1)
        if ONWARD[half][k] == 1:
            go(x_copy(arr, half, k, 2, slot(3), plus))
        else:
            go(x_copy(arr, half, k, 2, slot(1), minus))
        go(s_copy(arr, half, k, 3))
        go(s_copy(arr, half, k, 1))

    def spread_last(arr, half, k):
        recv_x(arr, half, k, 2)
        go(s_copy(arr, half, k, 2))

    def attend(arr, half, k):
        for steps in range(4):
            s_copy(arr, half, k, steps, 1).wait_recv()
        first, count = STARTS[half][k], CHUNKS[half][k]
        own = units[1 - arr, OWN, :, mine].reshape(ROWS, WIDTH)
        keys = units[arr, half, pl.ds(first, count)].reshape(count * 8 * GRAIN, WIDTH)
        logits = scale * lax.dot_general(own, keys, LAST, preferred_element_type=F32) + bias
        weight = jax.nn.sigmoid(logits)
        if half == OWN:
            row = lax.broadcasted_iota(jnp.int32, weight.shape, 0)
            col = lax.broadcasted_iota(jnp.int32, weight.shape, 1)
            grain = row // GRAIN
            match = (grain - first) * (8 * GRAIN) + mine * GRAIN + (row - grain * GRAIN)
            on = (col == match) & (grain >= first) & (grain < first + count)
            weight = weight - jnp.where(on, 1.0, 0.0)
        weight = weight.astype(BF16)
        acc[arr] += scale * jnp.dot(weight, keys, preferred_element_type=F32)

    crossing = [(arr, k) for arr in (TXT, IMG) for k in range(COUNT)]

    def arrive(i):
        z_copy(*crossing[i]).wait_recv()
        if i == IMAGES_AFTER:
            for k in range(COUNT):
                go(z_copy(IMG, k))
        spread_own(crossing[i][0], FAR, crossing[i][1])

    def rows_of(who, j):
        return pl.ds(pl.multiple_of(who * 576 + j * BLOCK_ROWS, 16), BLOCK_ROWS)

    def half_copy(j):
        return remote(theirs.at[j], s_buf.at[j], c_send.at[j], c_recv.at[j], sibling)

    def product(who, j):
        return jnp.dot(normed_t[rows_of(who, j)], back_ref[...], preferred_element_type=F32) * (1.0 / PAIRS)

    def image_back():
        img_back = acc[TXT]
        img_dir = img_dir_ref[...]
        back_ref[...] = ((img_back - img_dir * row_sum(img_dir * img_back)) * row_ref[2][:, :1]).astype(BF16)
        for j in range(4):
            theirs[j] = product(1 - core, j).astype(BF16)
            go(half_copy(j))

    def y_rows(d):
        return pl.ds(pl.multiple_of(((y + d) % 4) * 32, 16), PIECE)

    low, high = pl.ds(0, CUT), pl.ds(CUT, REST)
    here = y_rows(0)

    def ya_copy(d):
        return remote(
            summed.at[:, y_rows(d), low], ya_buf.at[d - 1], ya_send.at[d - 1], ya_recv.at[d - 1], y_peers[d - 1]
        )

    def xb_copy(d):
        return remote(
            summed.at[(x + d) % 4, :, high], xb_buf.at[d - 1], xb_send.at[d - 1], xb_recv.at[d - 1], x_peers[d - 1]
        )

    def first_sums():
        for j in range(4):
            own = product(core, j)
            half_copy(j).wait_recv()
            summed[j] = (own + s_buf[j].astype(F32)).astype(BF16)
        for d in (2, 1, 3):
            go(ya_copy(d))
            go(xb_copy(d))

    def norm_back():
        value = lax.dot_general(back_ref[...], proj_ref[...], LAST, preferred_element_type=F32)
        xhat = xhat_ref[...]
        terms = jnp.sum(value * xhat, axis=0, keepdims=True) * (1.0 / PAIRS)
        for i in range(9):
            g_sum[0, pl.ds(i, 1)] = terms[:, 128 * i : 128 * (i + 1)]
        go(g_copies(0)[0])
        scaled = value * gain_ref[...].reshape(1, WIDTH)
        mean = row_sum(scaled) * (1.0 / WIDTH)
        along = row_sum(scaled * xhat) * (1.0 / WIDTH)
        feature_out[...] = (row_ref[1][:, :1] * (scaled - mean - xhat * along)).astype(BF16)

    def xa_copy(d):
        return remote(ya_sum.at[(x + d) % 4], xa_buf.at[d - 1], xa_send.at[d - 1], xa_recv.at[d - 1], x_peers[d - 1])

    def yb_copy(d):
        return remote(xb_sum.at[y_rows(d)], yb_buf.at[d - 1], yb_send.at[d - 1], yb_recv.at[d - 1], y_peers[d - 1])

    def second_sums_b():
        total = summed[x, :, high].astype(F32)
        for d in (1, 2, 3):
            xb_copy(d).wait_recv()
            total = total + xb_buf[d - 1].astype(F32)
        xb_sum[...] = total.astype(BF16)
        for d in (2, 1, 3):
            go(yb_copy(d))

    def second_sums_a():
        for d in (1, 2, 3):
            ya_copy(d).wait_recv()
        for j in range(4):
            total = summed[j, here, low].astype(F32)
            for d in (1, 2, 3):
                total = total + ya_buf[d - 1, j].astype(F32)
            ya_sum[j] = total.astype(BF16)
        for d in (2, 1, 3):
            go(xa_copy(d))

    holder = core * 4 + x

    def h_copy(half, away):
        cols = low if half == 0 else high
        size = CUT if half == 0 else REST
        return remote(
            part.at[:, cols], z_buf.at[away - 1, :, pl.ds(0, size)], h_send.at[half], h_recv.at[away - 1],
            device(x, y, holder + 8 * half, core),
        )

    def away_from(half):
        return (z - holder - 8 * half + 32) % 16

    def to_holder(half):
        away = away_from(half)

        @pl.when(away != 0)
        def _():
            h_copy(half, away).start()

    def third_sums_b():
        total = xb_sum[here].astype(F32)
        for d in (1, 2, 3):
            yb_copy(d).wait_recv()
            total = total + yb_buf[d - 1].astype(F32)
        part[:, high] = total.astype(BF16)
        to_holder(1)

    def third_sums_a():
        total = ya_sum[x].astype(F32)
        for d in (1, 2, 3):
            xa_copy(d).wait_recv()
            total = total + xa_buf[d - 1].astype(F32)
        part[:, low] = total.astype(BF16)
        to_holder(0)

    is_holder = (z % 8) == holder
    on_root_core = core == (z % 8) // 4

    def cross_copy(half):
        cols = low if half == 0 else high
        return remote(gathered.at[:, cols], gathered.at[:, cols], b_send.at[0], b_recv.at[0], far)

    def row_copy(i):
        return remote(gathered, gathered, b_send.at[1 + i], b_recv.at[1], x_peers[i])

    def core_copy():
        return remote(gathered, gathered, b_send.at[4], b_recv.at[1], sibling)

    def holder_sums():
        for half in (0, 1):

            @pl.when(is_holder & (z // 8 == half))
            def _():
                size = CUT if half == 0 else REST
                cols = low if half == 0 else high
                total = part[:, cols].astype(F32)
                for away in range(1, 16):
                    h_copy(half, away).wait_recv()
                    total = total + z_buf[away - 1, :, pl.ds(0, size)].astype(F32)
                gathered[:, cols] = total.astype(BF16)
                cross_copy(half).start()

    def holder_rows():
        for half in (0, 1):

            @pl.when(is_holder & (z // 8 == half))
            def _():
                cross_copy(1 - half).wait_recv()
                cross_copy(half).wait_send()

        @pl.when(is_holder)
        def _():
            for i in (1, 0, 2):
                row_copy(i).start()
            core_copy().start()

    def spread_rows():
        @pl.when(jnp.logical_not(is_holder))
        def _():
            row_copy(0).wait_recv()

        @pl.when(on_root_core & jnp.logical_not(is_holder))
        def _():
            core_copy().start()

        for p in range(4):

            @pl.when(y == p)
            def _():
                grad_out[...] = gathered[...].astype(F32)[4 * p : 4 * p + WIDTH // 32]

    stages = [([sibling], 0), (y_peers, 1), (x_peers, 4), (z_peers, 7)]

    def g_copies(stage):
        peers, base = stages[stage]
        return [
            remote(g_sum.at[stage], g_buf.at[base + i], g_send.at[base + i], g_recv.at[base + i], peer)
            for i, peer in enumerate(peers)
        ]

    def g_total(stage):
        total = g_sum[stage]
        for i, copy in enumerate(g_copies(stage)):
            copy.wait_recv()
            total = total + g_buf[stages[stage][1] + i]
        g_sum[stage + 1] = total

    def g_next(stage):
        g_total(stage)
        if stage < 2:
            for copy in g_copies(stage + 1):
                go(copy)
        else:

            @pl.when(core == 0)
            def _():
                for copy in g_copies(3):
                    copy.start()

    def g_core_copy():
        return remote(g_sum.at[4], g_sum.at[4], g_send.at[22], g_recv.at[22], sibling)

    def g_along_z():
        @pl.when(core == 0)
        def _():
            g_total(3)
            g_core_copy().start()

    def g_finish():
        @pl.when(core == 1)
        def _():
            g_core_copy().wait_recv()

        for i in range(9):
            gain_out[pl.ds(128 * i, 128)] = g_sum[4, i]

    def text_back():
        txt_back = acc[IMG]
        txt_dir = txt_dir_ref[...]
        text_out[...] = ((txt_back - txt_dir * row_sum(txt_dir * txt_back)) * row_ref[0][:, :1]).astype(BF16)

    def text_units():
        values = text_ref[...].astype(F32)
        txt_inv = lax.rsqrt(row_sum(values * values) + 1e-6)
        txt_dir = values * txt_inv
        txt_dir_ref[...] = txt_dir
        units[TXT, OWN, :, mine] = txt_dir.astype(BF16).reshape(GRAINS, GRAIN, WIDTH)
        row_ref[0] = jnp.broadcast_to(txt_inv, (ROWS, 128))

    def image_units():
        values = feat_ref[...].astype(F32)
        centred = values - row_sum(values) * (1.0 / WIDTH)
        deviation = lax.rsqrt(row_sum(centred * centred) * (1.0 / WIDTH) + 1e-6)
        row_ref[1] = jnp.broadcast_to(deviation, (ROWS, 128))
        xhat = centred * deviation
        xhat_ref[...] = xhat
        normed_ref[...] = (xhat * gain_ref[...].reshape(1, WIDTH)).astype(BF16)
        projected = jnp.dot(normed_ref[...], proj_ref[...], preferred_element_type=F32)
        img_inv = lax.rsqrt(row_sum(projected * projected) + 1e-6)
        row_ref[2] = jnp.broadcast_to(img_inv, (ROWS, 128))
        img_dir = projected * img_inv
        img_dir_ref[...] = img_dir
        units[IMG, OWN, :, mine] = img_dir.astype(BF16).reshape(GRAINS, GRAIN, WIDTH)

    def transpose_normed():
        normed_t[...] = normed_ref[...].T

    acc[...] = jnp.zeros_like(acc)
    text_units()
    finish_barrier()
    for k in range(COUNT):
        go(z_copy(TXT, k))
    for k in range(OWN_COUNT):
        spread_own(TXT, OWN, k)
    image_units()
    for k in range(OWN_COUNT):
        spread_own(IMG, OWN, k)

    plan = [(5.0, transpose_normed, ())]

    def chain(arr, half, k, neighbours, last, pairs):
        plan.append((neighbours, spread_neighbours, (arr, half, k)))
        plan.append((last, spread_last, (arr, half, k)))
        plan.append((pairs, attend, (arr, half, k)))

    for k in range(OWN_COUNT):
        chain(TXT, OWN, k, *TXT_OWN[k])
        chain(IMG, OWN, k, *IMG_OWN[k])
    for k in range(COUNT):
        for arr in (TXT, IMG):
            times = FAR_TIMES[arr][k]
            plan.append((times[0], arrive, (arr * COUNT + k,)))
            chain(arr, FAR, k, *times[1:])
    tail = [
        image_back, first_sums, norm_back, second_sums_b, second_sums_a, third_sums_b, third_sums_a,
        holder_sums, holder_rows, spread_rows,
    ]
    for time, work in zip(TAIL, tail):
        plan.append((time, work, ()))
    for stage in range(3):
        plan.append((GAIN_TIMES[stage], g_next, (stage,)))
    plan.append((GAIN_TIMES[3], g_along_z, ()))
    plan.append((GAIN_TIMES[4], g_finish, ()))
    plan.append((200.0, text_back, ()))

    def drain(fraction):
        for _ in range(int(len(started) * fraction)):
            started.pop(0).wait_send()

    for time, fraction in DRAINS:
        plan.append((time, drain, (fraction,)))
    for _, work, args in sorted(plan, key=lambda entry: entry[0]):
        work(*args)

    drain(1.0)
    for half in (0, 1):
        away = away_from(half)

        @pl.when(away != 0)
        def _():
            h_copy(half, away).wait_send()

    @pl.when(is_holder)
    def _():
        for i in range(3):
            row_copy(i).wait_send()

    @pl.when(on_root_core)
    def _():
        core_copy().wait_send()

    @pl.when(core == 0)
    def _():
        for copy in g_copies(3):
            copy.wait_send()
        g_core_copy().wait_send()


def local(features, text, proj, gain, scale, bias):
    vmem = pl.BlockSpec(memory_space=pltpu.VMEM)
    smem = pl.BlockSpec(memory_space=pltpu.SMEM)
    dma = pltpu.SemaphoreType.DMA
    feature_grad, text_grad, grad, gain_gradient = pl.pallas_call(
        pair_kernel,
        out_shape=[
            jax.ShapeDtypeStruct((ROWS, WIDTH), BF16),
            jax.ShapeDtypeStruct((ROWS, WIDTH), BF16),
            jax.ShapeDtypeStruct((WIDTH // 32, WIDTH), F32),
            jax.ShapeDtypeStruct((WIDTH,), F32),
        ],
        in_specs=[vmem] * 4 + [smem] * 2,
        out_specs=[vmem] * 4,
        scratch_shapes=[
            pltpu.VMEM((2, 2, GRAINS, 8, GRAIN, WIDTH), BF16),
            pltpu.VMEM((2, ROWS, WIDTH), F32),
            pltpu.VMEM((ROWS, WIDTH), F32),
            pltpu.VMEM((ROWS, WIDTH), BF16),
            pltpu.VMEM((WIDTH, ROWS), BF16),
            pltpu.VMEM((ROWS, WIDTH), F32),
            pltpu.VMEM((ROWS, WIDTH), F32),
            pltpu.VMEM((3, ROWS, 128), F32),
            pltpu.VMEM((ROWS, WIDTH), BF16),
            pltpu.VMEM((4, BLOCK_ROWS, WIDTH), BF16),
            pltpu.VMEM((4, BLOCK_ROWS, WIDTH), BF16),
            pltpu.VMEM((4, BLOCK_ROWS, WIDTH), BF16),
            pltpu.VMEM((3, 4, PIECE, CUT), BF16),
            pltpu.VMEM((4, PIECE, CUT), BF16),
            pltpu.VMEM((3, BLOCK_ROWS, REST), BF16),
            pltpu.VMEM((BLOCK_ROWS, REST), BF16),
            pltpu.VMEM((3, PIECE, CUT), BF16),
            pltpu.VMEM((3, PIECE, REST), BF16),
            pltpu.VMEM((PIECE, WIDTH), BF16),
            pltpu.VMEM((15, PIECE, REST), BF16),
            pltpu.VMEM((PIECE, WIDTH), BF16),
            pltpu.VMEM((5, 9, 128), F32),
            pltpu.VMEM((22, 9, 128), F32),
            dma((2, 2, COUNT, 4)),
            dma((2, 2, COUNT, 4)),
            dma((2, 2, COUNT, 4)),
            dma((2, 2, COUNT, 4)),
            dma((2, COUNT)),
            dma((2, COUNT)),
            dma((4,)),
            dma((4,)),
            dma((3,)),
            dma((3,)),
            dma((3,)),
            dma((3,)),
            dma((3,)),
            dma((3,)),
            dma((3,)),
            dma((3,)),
            dma((2,)),
            dma((15,)),
            dma((5,)),
            dma((2,)),
            dma((23,)),
            dma((23,)),
        ],
        compiler_params=pltpu.CompilerParams(
            collective_id=0, has_side_effects=True, vmem_limit_bytes=34 * 2**20
        ),
        name="pairs",
    )(features[:, 0, :], text[:, 0, :], proj, gain, scale, bias)
    return feature_grad[:, None, :], text_grad[:, None, :], grad, gain_gradient

def solution(mesh):
    return jax.shard_map(
        local,
        mesh=mesh,
        in_specs=(P("loop", "rep", None), P("loop", "rep", None), P(), P(), P(), P()),
        out_specs=(P("loop", "rep", None), P("loop", "rep", None), P("rep", None), P()),
        check_vma=False,
    )
```

```python
import functools

import jax
import jax.numpy as jnp
from jax import lax
from jax.experimental import pallas as pl
from jax.experimental.pallas import tpu as pltpu
from jax.sharding import PartitionSpec as P

MESH = pl.DeviceIdType.MESH
WIDTH = 1152
ROWS = 192
GRAIN = 16
GRAINS = ROWS // GRAIN
CHUNKS = ((6, 6), (5, 5, 2))
STARTS = ((0, 6), (0, 5, 10))
OWN_COUNT, COUNT = len(CHUNKS[0]), len(CHUNKS[1])
PAIRS = 3072
TXT, IMG = 0, 1
OWN, FAR = 0, 1
IMAGES_AFTER = 1
BLOCK_ROWS = 144
PIECE = 48
CUT = 512
REST = WIDTH - CUT
LAST = (((1,), (1,)), ((), ()))
FIRST = (((0,), (0,)), ((), ()))
F32 = jnp.float32
BF16 = jnp.bfloat16


def coordinates():
    loop = lax.axis_index("loop")
    rep = lax.axis_index("rep")
    x = (loop // 2) % 4
    core = loop % 2
    z = (loop // 8) * 8 + rep // 4
    y = rep % 4
    return x, y, z, core


def device(x, y, z, core):
    x = (x + 4) % 4
    y = (y + 4) % 4
    z = (z + 32) % 16
    return ((z // 8) * 8 + x * 2 + core, (z % 8) * 4 + y)


def remote(src, dst, send_sem, recv_sem, target):
    return pltpu.make_async_remote_copy(
        src_ref=src,
        dst_ref=dst,
        send_sem=send_sem,
        recv_sem=recv_sem,
        device_id=target,
        device_id_type=MESH,
    )


def greet(peers):
    barrier = pltpu.get_barrier_semaphore()
    for peer in peers:
        pl.semaphore_signal(barrier, 1, device_id=peer, device_id_type=MESH)
    return lambda: pl.semaphore_wait(barrier, len(peers))


def row_sum(values):
    return jnp.sum(values, axis=-1, keepdims=True)

ONWARD = ((1, -1), (1, -1, 1))
TXT_OWN = ((6.0, 22.0, 30.5), (11.0, 23.0, 33.0))
IMG_OWN = ((16.0, 61.0, 63.1), (21.0, 61.1, 64.1))
FAR_TIMES = (
    ((27.0, 32.0, 36.0, 39.5), (34.0, 39.0, 43.2, 47.5), (43.0, 46.0, 49.0, 50.0)),
    ((67.4, 72.5, 76.0, 79.5), (72.3, 77.5, 81.0, 83.5), (77.0, 80.5, 84.0, 86.0)),
)
DRAINS = ((63.0, 0.6), (78.6, 0.8))
TAIL = (53.0, 58.0, 60.0, 66.0, 67.0, 71.0, 72.0, 80.0, 83.0, 87.0)
GAIN_TIMES = (62.5, 67.5, 72.2, 86.5, 88.0)


def pair_kernel(
    feat_hbm, text_hbm, proj_hbm, gain_ref, scale_ref, bias_ref,
    feature_out, text_out, grad_out, gain_out,
    units, acc, xhat_ref, normed_ref, normed_t, img_dir_ref, txt_dir_ref, row_ref, back_ref,
    theirs, summed, s_buf, ya_buf, ya_sum, xb_buf, xb_sum, xa_buf, yb_buf, part, z_buf, gathered, g_sum, g_buf,
    x_send, x_recv, s_send, s_recv, z_send, z_recv,
    c_send, c_recv, ya_send, ya_recv, xb_send, xb_recv, xa_send, xa_recv, yb_send, yb_recv,
    h_send, h_recv, b_send, b_recv, g_send, g_recv, feat_ref, text_ref, proj_ref, load_sem,
):
    x, y, z, core = coordinates()
    mine = x * 2 + core
    sibling = device(x, y, z, 1 - core)
    plus, minus = device(x + 1, y, z, core), device(x - 1, y, z, core)
    x_peers = [plus, device(x + 2, y, z, core), minus]
    y_peers = [device(x, y + d, z, core) for d in (1, 2, 3)]
    z_peers = [device(x, y, z + d, core) for d in range(1, 16)]
    far = z_peers[7]
    finish_barrier = greet([sibling] + x_peers + y_peers + z_peers)
    loads = [
        pltpu.make_async_copy(src, dst, load_sem.at[i])
        for i, (src, dst) in enumerate(((text_hbm, text_ref), (feat_hbm, feat_ref), (proj_hbm, proj_ref)))
    ]
    for load in loads:
        load.start()
    scale = scale_ref[0]
    bias = bias_ref[0]
    started = []

    def go(copy):
        copy.start()
        started.append(copy)

    def slot(steps, other=0):
        owner_core = core if other == 0 else 1 - core
        return ((x + steps) % 4) * 2 + owner_core

    def block(arr, half, k, where):
        return units.at[arr, half, pl.ds(STARTS[half][k], CHUNKS[half][k]), where]

    def x_copy(arr, half, k, steps, where, target):
        ref = block(arr, half, k, where)
        return remote(ref, ref, x_send.at[arr, half, k, steps], x_recv.at[arr, half, k, steps], target)

    def s_copy(arr, half, k, steps, from_sibling=0):
        ref = block(arr, half, k, slot(steps, from_sibling))
        return remote(ref, ref, s_send.at[arr, half, k, steps], s_recv.at[arr, half, k, steps], sibling)

    def z_copy(arr, k):
        src = units.at[arr, OWN, pl.ds(STARTS[FAR][k], CHUNKS[FAR][k]), mine]
        return remote(src, block(arr, FAR, k, mine), z_send.at[arr, k], z_recv.at[arr, k], far)

    def recv_x(arr, half, k, steps):
        x_copy(arr, half, k, steps, slot(steps), plus).wait_recv()

    def spread_own(arr, half, k):
        go(x_copy(arr, half, k, 3, mine, plus))
        go(x_copy(arr, half, k, 1, mine, minus))
        go(s_copy(arr, half, k, 0))

    def spread_neighbours(arr, half, k):
        recv_x(arr, half, k, 3)
        recv_x(arr, half, k, 1)
        if ONWARD[half][k] == 1:
            go(x_copy(arr, half, k, 2, slot(3), plus))
        else:
            go(x_copy(arr, half, k, 2, slot(1), minus))
        go(s_copy(arr, half, k, 3))
        go(s_copy(arr, half, k, 1))

    def spread_last(arr, half, k):
        recv_x(arr, half, k, 2)
        go(s_copy(arr, half, k, 2))

    def attend(arr, half, k):
        for steps in range(4):
            s_copy(arr, half, k, steps, 1).wait_recv()
        first, count = STARTS[half][k], CHUNKS[half][k]
        own = units[1 - arr, OWN, :, mine].reshape(ROWS, WIDTH)
        keys = units[arr, half, pl.ds(first, count)].reshape(count * 8 * GRAIN, WIDTH)
        logits = scale * lax.dot_general(own, keys, LAST, preferred_element_type=F32) + bias
        weight = jax.nn.sigmoid(logits)
        if half == OWN:
            row = lax.broadcasted_iota(jnp.int32, weight.shape, 0)
            col = lax.broadcasted_iota(jnp.int32, weight.shape, 1)
            grain = row // GRAIN
            match = (grain - first) * (8 * GRAIN) + mine * GRAIN + (row - grain * GRAIN)
            on = (col == match) & (grain >= first) & (grain < first + count)
            weight = weight - jnp.where(on, 1.0, 0.0)
        weight = weight.astype(BF16)
        acc[arr] += scale * jnp.dot(weight, keys, preferred_element_type=F32)

    crossing = [(arr, k) for arr in (TXT, IMG) for k in range(COUNT)]

    def arrive(i):
        z_copy(*crossing[i]).wait_recv()
        if i == IMAGES_AFTER:
            for k in range(COUNT):
                go(z_copy(IMG, k))
        spread_own(crossing[i][0], FAR, crossing[i][1])

    def rows_of(who, j):
        return pl.ds(pl.multiple_of(who * 576 + j * BLOCK_ROWS, 16), BLOCK_ROWS)

    def half_copy(j):
        return remote(theirs.at[j], s_buf.at[j], c_send.at[j], c_recv.at[j], sibling)

    def product(who, j):
        return jnp.dot(normed_t[rows_of(who, j)], back_ref[...], preferred_element_type=F32) * (1.0 / PAIRS)

    def image_back():
        img_back = acc[TXT]
        img_dir = img_dir_ref[...]
        back_ref[...] = ((img_back - img_dir * row_sum(img_dir * img_back)) * row_ref[2][:, :1]).astype(BF16)
        for j in range(4):
            theirs[j] = product(1 - core, j).astype(BF16)
            go(half_copy(j))

    def y_rows(d):
        return pl.ds(pl.multiple_of(((y + d) % 4) * 32, 16), PIECE)

    low, high = pl.ds(0, CUT), pl.ds(CUT, REST)
    here = y_rows(0)

    def ya_copy(d):
        return remote(
            summed.at[:, y_rows(d), low], ya_buf.at[d - 1], ya_send.at[d - 1], ya_recv.at[d - 1], y_peers[d - 1]
        )

    def xb_copy(d):
        return remote(
            summed.at[(x + d) % 4, :, high], xb_buf.at[d - 1], xb_send.at[d - 1], xb_recv.at[d - 1], x_peers[d - 1]
        )

    def first_sums():
        for j in range(4):
            own = product(core, j)
            half_copy(j).wait_recv()
            summed[j] = (own + s_buf[j].astype(F32)).astype(BF16)
        for d in (2, 1, 3):
            go(ya_copy(d))
            go(xb_copy(d))

    def norm_back():
        value = lax.dot_general(back_ref[...], proj_ref[...], LAST, preferred_element_type=F32)
        xhat = xhat_ref[...]
        terms = jnp.sum(value * xhat, axis=0, keepdims=True) * (1.0 / PAIRS)
        for i in range(9):
            g_sum[0, pl.ds(i, 1)] = terms[:, 128 * i : 128 * (i + 1)]
        go(g_copies(0)[0])
        scaled = value * gain_ref[...].reshape(1, WIDTH)
        mean = row_sum(scaled) * (1.0 / WIDTH)
        along = row_sum(scaled * xhat) * (1.0 / WIDTH)
        feature_out[...] = (row_ref[1][:, :1] * (scaled - mean - xhat * along)).astype(BF16)

    def xa_copy(d):
        return remote(ya_sum.at[(x + d) % 4], xa_buf.at[d - 1], xa_send.at[d - 1], xa_recv.at[d - 1], x_peers[d - 1])

    def yb_copy(d):
        return remote(xb_sum.at[y_rows(d)], yb_buf.at[d - 1], yb_send.at[d - 1], yb_recv.at[d - 1], y_peers[d - 1])

    def second_sums_b():
        total = summed[x, :, high].astype(F32)
        for d in (1, 2, 3):
            xb_copy(d).wait_recv()
            total = total + xb_buf[d - 1].astype(F32)
        xb_sum[...] = total.astype(BF16)
        for d in (2, 1, 3):
            go(yb_copy(d))

    def second_sums_a():
        for d in (1, 2, 3):
            ya_copy(d).wait_recv()
        for j in range(4):
            total = summed[j, here, low].astype(F32)
            for d in (1, 2, 3):
                total = total + ya_buf[d - 1, j].astype(F32)
            ya_sum[j] = total.astype(BF16)
        for d in (2, 1, 3):
            go(xa_copy(d))

    holder = core * 4 + x

    def h_copy(half, away):
        cols = low if half == 0 else high
        size = CUT if half == 0 else REST
        return remote(
            part.at[:, cols], z_buf.at[away - 1, :, pl.ds(0, size)], h_send.at[half], h_recv.at[away - 1],
            device(x, y, holder + 8 * half, core),
        )

    def away_from(half):
        return (z - holder - 8 * half + 32) % 16

    def to_holder(half):
        away = away_from(half)

        @pl.when(away != 0)
        def _():
            h_copy(half, away).start()

    def third_sums_b():
        total = xb_sum[here].astype(F32)
        for d in (1, 2, 3):
            yb_copy(d).wait_recv()
            total = total + yb_buf[d - 1].astype(F32)
        part[:, high] = total.astype(BF16)
        to_holder(1)

    def third_sums_a():
        total = ya_sum[x].astype(F32)
        for d in (1, 2, 3):
            xa_copy(d).wait_recv()
            total = total + xa_buf[d - 1].astype(F32)
        part[:, low] = total.astype(BF16)
        to_holder(0)

    is_holder = (z % 8) == holder
    on_root_core = core == (z % 8) // 4

    def cross_copy(half):
        cols = low if half == 0 else high
        return remote(gathered.at[:, cols], gathered.at[:, cols], b_send.at[0], b_recv.at[0], far)

    def row_copy(i):
        return remote(gathered, gathered, b_send.at[1 + i], b_recv.at[1], x_peers[i])

    def core_copy():
        return remote(gathered, gathered, b_send.at[4], b_recv.at[1], sibling)

    def holder_sums():
        for half in (0, 1):

            @pl.when(is_holder & (z // 8 == half))
            def _():
                size = CUT if half == 0 else REST
                cols = low if half == 0 else high
                total = part[:, cols].astype(F32)
                for away in range(1, 16):
                    h_copy(half, away).wait_recv()
                    total = total + z_buf[away - 1, :, pl.ds(0, size)].astype(F32)
                gathered[:, cols] = total.astype(BF16)
                cross_copy(half).start()

    def holder_rows():
        for half in (0, 1):

            @pl.when(is_holder & (z // 8 == half))
            def _():
                cross_copy(1 - half).wait_recv()
                cross_copy(half).wait_send()

        @pl.when(is_holder)
        def _():
            for i in (1, 0, 2):
                row_copy(i).start()
            core_copy().start()

    def spread_rows():
        @pl.when(jnp.logical_not(is_holder))
        def _():
            row_copy(0).wait_recv()

        @pl.when(on_root_core & jnp.logical_not(is_holder))
        def _():
            core_copy().start()

        for p in range(4):

            @pl.when(y == p)
            def _():
                grad_out[...] = gathered[...].astype(F32)[4 * p : 4 * p + WIDTH // 32]

    stages = [([sibling], 0), (y_peers, 1), (x_peers, 4), (z_peers, 7)]

    def g_copies(stage):
        peers, base = stages[stage]
        return [
            remote(g_sum.at[stage], g_buf.at[base + i], g_send.at[base + i], g_recv.at[base + i], peer)
            for i, peer in enumerate(peers)
        ]

    def g_total(stage):
        total = g_sum[stage]
        for i, copy in enumerate(g_copies(stage)):
            copy.wait_recv()
            total = total + g_buf[stages[stage][1] + i]
        g_sum[stage + 1] = total

    def g_next(stage):
        g_total(stage)
        if stage < 2:
            for copy in g_copies(stage + 1):
                go(copy)
        else:

            @pl.when(core == 0)
            def _():
                for copy in g_copies(3):
                    copy.start()

    def g_core_copy():
        return remote(g_sum.at[4], g_sum.at[4], g_send.at[22], g_recv.at[22], sibling)

    def g_along_z():
        @pl.when(core == 0)
        def _():
            g_total(3)
            g_core_copy().start()

    def g_finish():
        @pl.when(core == 1)
        def _():
            g_core_copy().wait_recv()

        for i in range(9):
            gain_out[pl.ds(128 * i, 128)] = g_sum[4, i]

    def text_back():
        txt_back = acc[IMG]
        txt_dir = txt_dir_ref[...]
        text_out[...] = ((txt_back - txt_dir * row_sum(txt_dir * txt_back)) * row_ref[0][:, :1]).astype(BF16)

    def text_units():
        values = text_ref[...].astype(F32)
        txt_inv = lax.rsqrt(row_sum(values * values) + 1e-6)
        txt_dir = values * txt_inv
        txt_dir_ref[...] = txt_dir
        units[TXT, OWN, :, mine] = txt_dir.astype(BF16).reshape(GRAINS, GRAIN, WIDTH)
        row_ref[0] = jnp.broadcast_to(txt_inv, (ROWS, 128))

    def image_units():
        values = feat_ref[...].astype(F32)
        centred = values - row_sum(values) * (1.0 / WIDTH)
        deviation = lax.rsqrt(row_sum(centred * centred) * (1.0 / WIDTH) + 1e-6)
        row_ref[1] = jnp.broadcast_to(deviation, (ROWS, 128))
        xhat = centred * deviation
        xhat_ref[...] = xhat
        normed_ref[...] = (xhat * gain_ref[...].reshape(1, WIDTH)).astype(BF16)
        projected = jnp.dot(normed_ref[...], proj_ref[...], preferred_element_type=F32)
        img_inv = lax.rsqrt(row_sum(projected * projected) + 1e-6)
        row_ref[2] = jnp.broadcast_to(img_inv, (ROWS, 128))
        img_dir = projected * img_inv
        img_dir_ref[...] = img_dir
        units[IMG, OWN, :, mine] = img_dir.astype(BF16).reshape(GRAINS, GRAIN, WIDTH)

    def transpose_normed():
        normed_t[...] = normed_ref[...].T

    acc[...] = jnp.zeros_like(acc)
    loads[0].wait()
    text_units()
    finish_barrier()
    for k in range(COUNT):
        go(z_copy(TXT, k))
    for k in range(OWN_COUNT):
        spread_own(TXT, OWN, k)
    loads[1].wait()
    loads[2].wait()
    image_units()
    for k in range(OWN_COUNT):
        spread_own(IMG, OWN, k)

    plan = [(5.0, transpose_normed, ())]

    def chain(arr, half, k, neighbours, last, pairs):
        plan.append((neighbours, spread_neighbours, (arr, half, k)))
        plan.append((last, spread_last, (arr, half, k)))
        plan.append((pairs, attend, (arr, half, k)))

    for k in range(OWN_COUNT):
        chain(TXT, OWN, k, *TXT_OWN[k])
        chain(IMG, OWN, k, *IMG_OWN[k])
    for k in range(COUNT):
        for arr in (TXT, IMG):
            times = FAR_TIMES[arr][k]
            plan.append((times[0], arrive, (arr * COUNT + k,)))
            chain(arr, FAR, k, *times[1:])
    tail = [
        image_back, first_sums, norm_back, second_sums_b, second_sums_a, third_sums_b, third_sums_a,
        holder_sums, holder_rows, spread_rows,
    ]
    for time, work in zip(TAIL, tail):
        plan.append((time, work, ()))
    for stage in range(3):
        plan.append((GAIN_TIMES[stage], g_next, (stage,)))
    plan.append((GAIN_TIMES[3], g_along_z, ()))
    plan.append((GAIN_TIMES[4], g_finish, ()))
    plan.append((200.0, text_back, ()))

    def drain(fraction):
        for _ in range(int(len(started) * fraction)):
            started.pop(0).wait_send()

    for time, fraction in DRAINS:
        plan.append((time, drain, (fraction,)))
    for _, work, args in sorted(plan, key=lambda entry: entry[0]):
        work(*args)

    drain(1.0)
    for half in (0, 1):
        away = away_from(half)

        @pl.when(away != 0)
        def _():
            h_copy(half, away).wait_send()

    @pl.when(is_holder)
    def _():
        for i in range(3):
            row_copy(i).wait_send()

    @pl.when(on_root_core)
    def _():
        core_copy().wait_send()

    @pl.when(core == 0)
    def _():
        for copy in g_copies(3):
            copy.wait_send()
        g_core_copy().wait_send()


def local(features, text, proj, gain, scale, bias):
    vmem = pl.BlockSpec(memory_space=pltpu.VMEM)
    smem = pl.BlockSpec(memory_space=pltpu.SMEM)
    hbm = pl.BlockSpec(memory_space=pltpu.HBM)
    dma = pltpu.SemaphoreType.DMA
    feature_grad, text_grad, grad, gain_gradient = pl.pallas_call(
        pair_kernel,
        out_shape=[
            jax.ShapeDtypeStruct((ROWS, WIDTH), BF16),
            jax.ShapeDtypeStruct((ROWS, WIDTH), BF16),
            jax.ShapeDtypeStruct((WIDTH // 32, WIDTH), F32),
            jax.ShapeDtypeStruct((WIDTH,), F32),
        ],
        in_specs=[hbm] * 3 + [vmem] + [smem] * 2,
        out_specs=[vmem] * 4,
        scratch_shapes=[
            pltpu.VMEM((2, 2, GRAINS, 8, GRAIN, WIDTH), BF16),
            pltpu.VMEM((2, ROWS, WIDTH), F32),
            pltpu.VMEM((ROWS, WIDTH), F32),
            pltpu.VMEM((ROWS, WIDTH), BF16),
            pltpu.VMEM((WIDTH, ROWS), BF16),
            pltpu.VMEM((ROWS, WIDTH), F32),
            pltpu.VMEM((ROWS, WIDTH), F32),
            pltpu.VMEM((3, ROWS, 128), F32),
            pltpu.VMEM((ROWS, WIDTH), BF16),
            pltpu.VMEM((4, BLOCK_ROWS, WIDTH), BF16),
            pltpu.VMEM((4, BLOCK_ROWS, WIDTH), BF16),
            pltpu.VMEM((4, BLOCK_ROWS, WIDTH), BF16),
            pltpu.VMEM((3, 4, PIECE, CUT), BF16),
            pltpu.VMEM((4, PIECE, CUT), BF16),
            pltpu.VMEM((3, BLOCK_ROWS, REST), BF16),
            pltpu.VMEM((BLOCK_ROWS, REST), BF16),
            pltpu.VMEM((3, PIECE, CUT), BF16),
            pltpu.VMEM((3, PIECE, REST), BF16),
            pltpu.VMEM((PIECE, WIDTH), BF16),
            pltpu.VMEM((15, PIECE, REST), BF16),
            pltpu.VMEM((PIECE, WIDTH), BF16),
            pltpu.VMEM((5, 9, 128), F32),
            pltpu.VMEM((22, 9, 128), F32),
            dma((2, 2, COUNT, 4)),
            dma((2, 2, COUNT, 4)),
            dma((2, 2, COUNT, 4)),
            dma((2, 2, COUNT, 4)),
            dma((2, COUNT)),
            dma((2, COUNT)),
            dma((4,)),
            dma((4,)),
            dma((3,)),
            dma((3,)),
            dma((3,)),
            dma((3,)),
            dma((3,)),
            dma((3,)),
            dma((3,)),
            dma((3,)),
            dma((2,)),
            dma((15,)),
            dma((5,)),
            dma((2,)),
            dma((23,)),
            dma((23,)),
            pltpu.VMEM((ROWS, WIDTH), BF16),
            pltpu.VMEM((ROWS, WIDTH), BF16),
            pltpu.VMEM((WIDTH, WIDTH), BF16),
            dma((3,)),
        ],
        compiler_params=pltpu.CompilerParams(
            collective_id=0, has_side_effects=True, vmem_limit_bytes=52 * 2**20
        ),
        name="pairs",
    )(features[:, 0, :], text[:, 0, :], proj, gain, scale, bias)
    return feature_grad[:, None, :], text_grad[:, None, :], grad, gain_gradient

def solution(mesh):
    return jax.shard_map(
        local,
        mesh=mesh,
        in_specs=(P("loop", "rep", None), P("loop", "rep", None), P(), P(), P(), P()),
        out_specs=(P("loop", "rep", None), P("loop", "rep", None), P("rep", None), P()),
        check_vma=False,
    )
```
